1024 devices in a mesh: grp: 8 (over x_lo, core), gx: 8 (over y), gy: 16 (over x_hi, z).
Axes of the slice: x: 8 (x_hi: 2, x_lo: 4; x = x_hi * 4 + x_lo), y: 8, z: 8, core: 2. Of those that a mesh axis runs over, the one named last changes fastest.
Arguments:
- state: float32 [3, 32, 512, 1024], P(None, 'grp', 'gy', 'gx'), may hold values from -6 to 6
- coefs: float32 [2, 32, 512, 1024], P(None, 'grp', 'gy', 'gx'), may hold values from 0.1 to 0.4
- lagged_absorbers: bfloat16 [7, 32, 512, 1024], P(None, 'grp', 'gy', 'gx'), may hold values from 0.049804688 to 1
- sun_route: int32 [512, 8], P('gy', 'gx'), may hold values from 0 to 16, as said below
- band_coef: bfloat16 [112, 7], replicated, may hold values from 0.0019989014 to 0.29882812
- solar: float32 [112], replicated, may hold values from 0.01 to 0.15
- layer_mass: float32 [32], replicated, may hold values from 0.5 to 2
- remap_index: int32 [32, 4], replicated, may hold values from 0 to 31, as said below
- remap_weight: float32 [32, 4], replicated, may hold values from 0.05 to 0.45
Outputs:
- new_state: float32 [3, 32, 512, 1024], P(None, 'grp', 'gy', 'gx')
- heating: float32 [32, 512, 1024], P('grp', 'gy', 'gx')
The draws below stay inside these ranges and needn't reach their ends.
Inputs may be any that keep to these rules, and one draw needn't show every extreme that they name: `sun_route`: the block of 128 columns in face row x and gx index y is sunlit where the value is below 16; the value then names one of the 16 radiation devices of the gy index that holds row x, counted with gx fastest over the last quarter of grp; the value 16 marks a dark block. Within the 32 rows of one gy index and one gx index at most 2 blocks name the same device, and in every draw some device is named by 2 blocks of every gx index of its gy index. `remap_index`: every entry lies within 2 levels of its row's level k; the first two taps are max(k - 2, 0) and min(k + 2, 31).
All inputs are finite; a program needn't handle non-finite values.
Results may differ from the reference program's by a relative error of at most 0.0003.
Values may be sent and summed in bfloat16 or wider, within the bound.
A program may use at most 32 MiB of HBM per device.

```python
import math
import jax
import jax.numpy as jnp
from jax import lax

TX = 32
TY = 128
F = 7
G = 112
SUB = 8
CAP = 2
RIM = 2
NTAP = 4
LEV = 32
LEV_DYN = 24
NXF = 512
NYF = 1024
NRAD = 16
N_GX = 8
N_GY = 16


def draw_sun_route(key, part):
    key = jax.random.fold_in(key, 11)
    tile_keys = jax.random.split(key, N_GY * N_GX)
    pool_values = jnp.concatenate([jnp.arange(NRAD * CAP, dtype=jnp.int32) // CAP, jnp.full((TX,), NRAD, jnp.int32)])

    def shuffle(tile_key):
        return jax.random.permutation(tile_key, pool_values)[:TX]
    tiles = jax.vmap(shuffle)(tile_keys).reshape(N_GY, N_GX, TX)
    chosen_device = jax.random.randint(jax.random.fold_in(key, 1), (), 0, NRAD)
    chosen_line = jax.random.randint(jax.random.fold_in(key, 2), (), 0, N_GY)
    in_line = (jnp.arange(N_GY) == chosen_line)[:, None, None]
    leading = (jnp.arange(TX) < CAP)[None, None, :]
    cleared = jnp.where(in_line & (tiles == chosen_device), NRAD, tiles)
    tiles = jnp.where(in_line & leading, chosen_device, cleared)
    return jnp.transpose(tiles, (0, 2, 1)).reshape(N_GY * TX, N_GX).astype(jnp.int32)


def draw_remap_index(key, part):
    key = jax.random.fold_in(key, 23)
    level_column = jnp.arange(LEV, dtype=jnp.int32)[:, None]
    offsets = jax.random.randint(key, (LEV, NTAP - 2), -RIM, RIM + 1).astype(jnp.int32)
    offsets = jnp.concatenate([jnp.full((LEV, 1), -RIM, jnp.int32), jnp.full((LEV, 1), RIM, jnp.int32), offsets], 1)
    return jnp.clip(level_column + offsets, 0, LEV - 1).astype(jnp.int32)


def levels(stream_key, shape, cuts, low, high):
    def one(position, shards_of):
        heights = jax.random.uniform(jax.random.fold_in(jax.random.fold_in(stream_key, 6), position), (shards_of,), jnp.float32, low / len(cuts), high / len(cuts))
        return jnp.repeat(jnp.exp(heights), shape[position] // shards_of).reshape((-1,) + (1,) * (len(shape) - position - 1))

    loudness = one(*cuts[0])
    for cut in cuts[1:]:
        loudness = loudness * one(*cut)
    return loudness


def normal_values(own_key, shape, spread, bound, shards=(), held_as=jnp.bfloat16):
    result = jax.random.normal(own_key, shape, jnp.float32) * spread
    if len(shards) > 0:
        result = levels(own_key, shape, shards, -0.22, 0.18) * result
    return jnp.clip(result, min=-bound, max=bound).astype(held_as)


def setup_inputs(seed: int = 0) -> dict:
    key_of = jax.random.split(jax.random.key(seed), 10)
    return {
        "state": normal_values(key_of[0], (3, LEV, NXF, NYF), 1.0, 6.0, ((1, 8), (2, 16), (3, 8)), jnp.float32),
        "coefs": jnp.clip(0.1 + 0.3 * jax.random.uniform(key_of[1], (2, LEV, NXF, NYF), jnp.float32) ** levels(key_of[1], (2, LEV, NXF, NYF), ((1, 8), (2, 16), (3, 8)), -0.2, 0.2), 0.1, 0.4),
        "lagged_absorbers": jnp.clip(jnp.exp(math.log(1.0) - 2.9996462 * jax.random.uniform(key_of[2], (F, LEV, NXF, NYF), jnp.float32) ** levels(key_of[2], (F, LEV, NXF, NYF), ((1, 8), (2, 16), (3, 8)), -0.2, 0.2)), 0.049804688, 1.0).astype(jnp.bfloat16),
        "sun_route": draw_sun_route(jax.random.fold_in(key_of[9], 71), 0),
        "band_coef": jnp.clip(jnp.exp(jax.random.uniform(key_of[4], (G, F), jnp.float32, math.log(0.0019989014), math.log(0.29882812))), 0.0019989014, 0.29882812).astype(jnp.bfloat16),
        "solar": jnp.clip(jnp.exp(jax.random.uniform(key_of[5], (G,), jnp.float32, math.log(0.01), math.log(0.15))), 0.01, 0.15),
        "layer_mass": jnp.clip(jnp.exp(jax.random.uniform(key_of[6], (LEV,), jnp.float32, math.log(0.5), math.log(2.0))), 0.5, 2.0),
        "remap_index": draw_remap_index(jax.random.fold_in(key_of[9], 71), 0),
        "remap_weight": jnp.clip(jax.random.uniform(key_of[8], (LEV, NTAP), jnp.float32, 0.05, 0.45), 0.05, 0.45),
    }


def padded(field):
    return jnp.pad(field, ((0, 0), (1, 1), (1, 1)))


def reference(state, coefs, lagged_absorbers, sun_route, band_coef, solar, layer_mass, remap_index, remap_weight):
    flow_x, flow_y, pressure = state[0], state[1], state[2]
    buoyancy, stiffness = coefs[0], coefs[1]
    for substep in range(SUB):
        beside_all = padded(pressure)
        flow_x = flow_x - buoyancy * (beside_all[:, 2:, 1:-1] - beside_all[:, :-2, 1:-1])
        flow_y = flow_y - buoyancy * (beside_all[:, 1:-1, 2:] - beside_all[:, 1:-1, :-2])
        wide_x = padded(flow_x)
        wide_y = padded(flow_y)
        pressure = pressure - stiffness * ((wide_x[:, 2:, 1:-1] - wide_x[:, :-2, 1:-1]) + (wide_y[:, 1:-1, 2:] - wide_y[:, 1:-1, :-2]))
    stepped = jnp.stack([flow_x, flow_y, pressure])
    moving = (jnp.arange(LEV) < LEV_DYN)[None, :, None, None]
    stepped = jnp.where(moving, stepped, state)
    new_state = jnp.zeros_like(stepped)
    for tap in range(NTAP):
        new_state = new_state + remap_weight[:, tap][None, :, None, None] * stepped[:, remap_index[:, tap]]
    band_wide = band_coef.astype(jnp.float32)
    top_flux = jnp.sum(solar)

    def one_row(inputs):
        gases, routes = inputs
        depth_in = jnp.cumsum(gases.astype(jnp.float32), axis=1)
        optical = jnp.einsum('gf,fkn->gkn', band_wide, depth_in, precision=lax.Precision.HIGHEST)
        flux = jnp.einsum('g,gkn->kn', solar, jnp.exp(-optical), precision=lax.Precision.HIGHEST)
        above = jnp.concatenate([jnp.broadcast_to(top_flux, (1, flux.shape[1])), flux[:-1]], 0)
        rates = (above - flux) / layer_mass[:, None]
        sunlit = jnp.repeat((routes < NRAD).astype(jnp.float32), TY)
        return rates * sunlit[None, :]

    rows = lax.map(one_row, (jnp.moveaxis(lagged_absorbers, 2, 0), sun_route))
    heating = jnp.transpose(rows, (1, 0, 2))
    return new_state, heating
```

```python
import functools

import jax
import jax.numpy as jnp
from jax import lax
from jax.experimental import pallas as pl
from jax.experimental.pallas import tpu as pltpu
from jax.sharding import PartitionSpec as P

SUB = 8
RIM = 2
H = 2 * SUB
NDARK = 16
MESH = pl.DeviceIdType.MESH
LOG2E = 1.4426950408889634


def lane_ids(rows):
    return lax.broadcasted_iota(jnp.int32, (rows, 128), 1)


def ahead(main, side, lane):
    m, s = pltpu.roll(main, 126, 1), pltpu.roll(side, 126, 1)
    keep = lane < 126
    return jnp.where(keep, m, s), jnp.where(keep, s, m)


def ahead1(main, side, lane):
    m, s = pltpu.roll(main, 127, 1), pltpu.roll(side, 127, 1)
    keep = lane < 127
    return jnp.where(keep, m, s), jnp.where(keep, s, m)


def behind(main, side, lane):
    m, s = pltpu.roll(main, 2, 1), pltpu.roll(side, 2, 1)
    keep = lane >= 2
    return jnp.where(keep, m, s), jnp.where(keep, s, m)


def substeps(p, fx, fy, b, s):
    rows = p[0].shape[0]
    lane = lane_ids(rows)

    def up(v, n):
        return tuple(pltpu.roll(a, a.shape[0] - n, 0) for a in v)

    def down(v, n):
        return tuple(pltpu.roll(a, n, 0) for a in v)

    fx, bx = up(fx, 1), up(b, 1)
    fy, by = ahead1(*fy, lane), ahead1(*b, lane)
    top = H
    for step in range(SUB):
        if step == SUB // 2:
            cut = lambda v: tuple(a[8 : rows - 8] for a in v)
            p, fx, fy, bx, by, s = cut(p), cut(fx), cut(fy), cut(bx), cut(by), cut(s)
            lane = lane_ids(rows - 16)
            top = H - 8
        px, py = up(p, 2), ahead(*p, lane)
        fx = tuple(f - c * (n - o) for f, c, n, o in zip(fx, bx, px, p))
        fy = tuple(f - c * (n - o) for f, c, n, o in zip(fy, by, py, p))
        gx, gy = down(fx, 2), behind(*fy, lane)
        p = tuple(
            o - c * ((x1 - x0) + (y1 - y0))
            for o, c, x1, x0, y1, y0 in zip(p, s, fx, gx, fy, gy)
        )
    fx = down(fx, 1)[0]
    fy0, fy1 = pltpu.roll(fy[0], 1, 1), pltpu.roll(fy[1], 1, 1)
    fy = jnp.where(lane >= 1, fy0, fy1)
    own = slice(top, top + rows - 2 * H)
    return fx[own], fy[own], p[0][own]


def kernel(
    sizes,
    state, coefs, absorbers, route, band, solar, mass, ridx, rweight,
    new_state, heating,
    tile, gas, send_r, send_l, from_l, from_r, ext, block_sum, sib, chip_sum, lower, part, rest, prefix, lhs,
    in_sem, send_sem, recv_sem,
):
    n_grp, n_gx, n_gy = sizes
    dyn_groups = 3 * n_grp // 4
    chips = n_grp // 2
    levels, rows = 4, 32
    me, gx, gy = lax.axis_index("grp"), lax.axis_index("gx"), lax.axis_index("gy")
    core, chip = lax.rem(me, 2), lax.div(me, 2)
    dyn = me < dyn_groups
    has_l, has_r = gx > 0, gx < n_gx - 1
    has_u, has_d = gy > 0, gy < n_gy - 1
    land = jnp.logical_and

    loads = [
        pltpu.make_async_copy(state, tile.at[0:3, :, H : H + rows, :], in_sem.at[0]),
        pltpu.make_async_copy(coefs, tile.at[3:5, :, H : H + rows, :], in_sem.at[1]),
        pltpu.make_async_copy(absorbers, gas, in_sem.at[2]),
    ]
    for load in loads:
        load.start()

    partners = []
    for dx, cx in ((-1, has_l), (0, None), (1, has_r)):
        for dy, cy in ((-1, has_u), (0, None), (1, has_d)):
            if dx == 0 and dy == 0:
                continue
            cond = dyn
            if cx is not None:
                cond = land(cond, cx)
            if cy is not None:
                cond = land(cond, cy)
            partners.append((cond, {"gx": gx + dx, "gy": gy + dy}))
    steps = sorted({1} | {2 * d for d in range(1, chips)})
    for d in steps:
        partners.append((me + d < n_grp, {"grp": me + d}))
        partners.append((me - d >= 0, {"grp": me - d}))
    barrier = pltpu.get_barrier_semaphore()
    count = jnp.int32(0)
    for cond, dev in partners:
        count = count + cond.astype(jnp.int32)

        @pl.when(cond)
        def _(dev=dev):
            pl.semaphore_signal(barrier, inc=1, device_id=dev, device_id_type=MESH)

    number = [0]

    def remote(src, dst, dev):
        i = number[0]
        number[0] += 1
        return pltpu.make_async_remote_copy(
            src_ref=src, dst_ref=dst, send_sem=send_sem.at[i], recv_sem=recv_sem.at[i], device_id=dev, device_id_type=MESH
        )

    def all_of(*conds):
        return functools.reduce(land, conds)

    halo = [
        (all_of(dyn, has_d), all_of(dyn, has_u), remote(tile.at[:, :, rows : rows + H], tile.at[:, :, 0:H], {"gy": gy + 1})),
        (all_of(dyn, has_u), all_of(dyn, has_d), remote(tile.at[:, :, H : 2 * H], tile.at[:, :, rows + H : rows + 2 * H], {"gy": gy - 1})),
        (all_of(dyn, has_r), all_of(dyn, has_l), remote(send_r, from_l.at[:, H : H + rows], {"gx": gx + 1})),
        (all_of(dyn, has_l), all_of(dyn, has_r), remote(send_l, from_r.at[:, H : H + rows], {"gx": gx - 1})),
        (all_of(dyn, has_r, has_d), all_of(dyn, has_l, has_u), remote(send_r.at[:, rows - H :], from_l.at[:, 0:H], {"gx": gx + 1, "gy": gy + 1})),
        (all_of(dyn, has_r, has_u), all_of(dyn, has_l, has_d), remote(send_r.at[:, 0:H], from_l.at[:, rows + H :], {"gx": gx + 1, "gy": gy - 1})),
        (all_of(dyn, has_l, has_d), all_of(dyn, has_r, has_u), remote(send_l.at[:, rows - H :], from_r.at[:, 0:H], {"gx": gx - 1, "gy": gy + 1})),
        (all_of(dyn, has_l, has_u), all_of(dyn, has_r, has_d), remote(send_l.at[:, 0:H], from_r.at[:, rows + H :], {"gx": gx - 1, "gy": gy - 1})),
    ]
    true = me >= 0
    half = rows // 2
    mine = pl.multiple_of(half * core, half)
    other = pl.multiple_of(half * (1 - core), half)
    sibling = {"grp": me + 1 - 2 * core}
    to_sib = remote(block_sum.at[:, pl.ds(other, half)], sib, sibling)
    to_chips = [
        (chip + d < chips, chip - d >= 0, remote(chip_sum, lower.at[d - 1], {"grp": me + 2 * d})) for d in range(1, chips)
    ]
    to_rest = remote(part, rest, sibling)
    remap = [
        (me > 0, me < n_grp - 1, remote(ext.at[:, RIM : 2 * RIM], ext.at[:, levels + RIM :], {"grp": me - 1})),
        (me < n_grp - 1, me > 0, remote(ext.at[:, levels : levels + RIM], ext.at[:, 0:RIM], {"grp": me + 1})),
    ]

    def start(item):
        @pl.when(item[0])
        def _():
            item[2].start()

    def wait_recv(item):
        @pl.when(item[1])
        def _():
            item[2].wait_recv()

    def wait_send(item):
        @pl.when(item[0])
        def _():
            item[2].wait_send()

    loads[0].wait()
    loads[1].wait()

    lane = lane_ids(rows)
    for q in range(3):
        right = jnp.zeros((rows, 128), jnp.float32)
        left = jnp.zeros((rows, 128), jnp.float32)
        for c in (2 * q, 2 * q + 1):
            if c > 4:
                continue
            for l in range(levels):
                t = 2 * l + c % 2
                cells = tile[c, l, H : H + rows, :]
                here = lax.div(lane, 16) == t
                shift = (16 * t + 16) % 128
                right = jnp.where(here, pltpu.roll(cells, shift, 1) if shift else cells, right)
                shift = 16 * t
                left = jnp.where(here, pltpu.roll(cells, shift, 1) if shift else cells, left)
        send_r[q] = right
        send_l[q] = left

    pl.semaphore_wait(barrier, count)
    for item in halo:
        start(item)

    loads[2].wait()
    for f in range(gas.shape[0]):
        total = gas[f, 0].astype(jnp.float32)
        for l in range(1, levels):
            total = total + gas[f, l].astype(jnp.float32)
        block_sum[f] = total
    to_sib.start()

    def fill(cond, ref, *index):
        @pl.when(cond)
        def _():
            view = ref.at[index] if index else ref
            view[...] = jnp.zeros(view.shape, view.dtype)

    fill(~has_u, tile, slice(None), slice(None), slice(0, H))
    fill(~has_d, tile, slice(None), slice(None), slice(rows + H, rows + 2 * H))
    fill(~has_l, from_l)
    fill(~has_r, from_r)
    fill(land(has_l, ~has_u), from_l, slice(None), slice(0, H))
    fill(land(has_l, ~has_d), from_l, slice(None), slice(rows + H, rows + 2 * H))
    fill(land(has_r, ~has_u), from_r, slice(None), slice(0, H))
    fill(land(has_r, ~has_d), from_r, slice(None), slice(rows + H, rows + 2 * H))
    fill(me == 0, ext, slice(None), slice(0, RIM))
    fill(me == n_grp - 1, ext, slice(None), slice(levels + RIM, levels + 2 * RIM))
    for d in range(1, chips):
        fill(chip - d < 0, lower, d - 1)

    @pl.when(~dyn)
    def _():
        for c in range(3):
            ext[c, RIM : RIM + levels] = tile[c, :, H : H + rows, :]

    gpoints, gases = band.shape
    r0 = lax.broadcasted_iota(jnp.int32, (gpoints, gpoints), 0)
    r1 = lax.broadcasted_iota(jnp.int32, (gpoints, gpoints), 1)
    column = jnp.sum(jnp.where(r0 == r1, jnp.broadcast_to(solar[...], (gpoints, gpoints)), 0.0), axis=1, keepdims=True)
    logs = jnp.log2(column)
    high = logs.astype(jnp.bfloat16).astype(jnp.float32)
    middle = (logs - high).astype(jnp.bfloat16).astype(jnp.float32)
    low = logs - high - middle
    srcs = jnp.concatenate([band[...].astype(jnp.float32), high, middle, low], axis=1).astype(jnp.bfloat16)
    n_src = gases + 3
    spread0 = lax.div(lax.broadcasted_iota(jnp.int32, (8 * gpoints, gpoints), 0), 8)
    spread1 = lax.broadcasted_iota(jnp.int32, (8 * gpoints, gpoints), 1)
    spread = (spread0 == spread1).astype(jnp.float32).astype(jnp.bfloat16)
    tall = jnp.dot(spread, srcs, preferred_element_type=jnp.float32).astype(jnp.bfloat16)
    w0 = lax.broadcasted_iota(jnp.int32, (n_src, 128), 0)
    w1 = lax.broadcasted_iota(jnp.int32, (n_src, 128), 1)
    in_gas = w1 < 16 * gases
    owner = jnp.where(in_gas, lax.rem(lax.div(w1, 8), gases), w1 - 16 * gases + gases)
    widen = (w0 == owner).astype(jnp.float32).astype(jnp.bfloat16)
    wide = jnp.dot(tall, widen, preferred_element_type=jnp.float32)
    m0 = lax.broadcasted_iota(jnp.int32, (8 * gpoints, 128), 0)
    m1 = lax.broadcasted_iota(jnp.int32, (8 * gpoints, 128), 1)
    keep = (m1 >= 16 * gases) | (lax.rem(m0, 8) == lax.rem(m1, 8))
    lhs[...] = jnp.where(keep, wide, 0.0).astype(jnp.bfloat16)

    to_sib.wait_recv()
    chip_sum[...] = block_sum[:, pl.ds(mine, half), :] + sib[...]
    for item in to_chips:
        start(item)

    for item in halo:
        wait_recv(item)

    @pl.when(dyn)
    def _():
        lane_w = lane_ids(rows + 2 * H)

        def level(i, carry):
            l = lax.rem(i + 2 * core, levels)

            def pair(c):
                t = 2 * l + c % 2
                left = pltpu.roll(from_l[c // 2], lax.rem(112 - 16 * t + 128, 128), 1)
                right = pltpu.roll(from_r[c // 2], lax.rem(128 - 16 * t, 128), 1)
                side = jnp.where(lane_w < 16, right, jnp.where(lane_w >= 112, left, 0.0))
                return tile[c, l], side

            out = substeps(pair(2), pair(0), pair(1), pair(3), pair(4))
            for c in range(3):
                ext[c, RIM + l] = out[c]
            return carry

        lax.fori_loop(0, levels, level, 0)

    for item in remap:
        start(item)

    for item in to_chips:
        wait_recv(item)
    above = lower[0]
    for d in range(2, chips):
        above = above + lower[d - 1]
    even = (core == 0).astype(jnp.float32)
    part[...] = above + even * block_sum[:, pl.ds(mine, half), :]
    to_rest.start()
    prefix[...] = above + (1.0 - even) * sib[...]

    def radiate(start_row, ref):
        columns = []
        for g in range(half // 8):
            depth = ref[:, 8 * g : 8 * g + 8, :]
            for l in range(levels + 1):
                if l:
                    cells = gas[:, l - 1, pl.ds(start_row, half), :].astype(jnp.float32)
                    depth = depth + cells[:, 8 * g : 8 * g + 8, :]
                scaled = (depth * -LOG2E).reshape(8 * gases, 128)
                high = scaled.astype(jnp.bfloat16).astype(jnp.float32)
                stack = jnp.concatenate([high, scaled - high, jnp.ones((128 - 16 * gases, 128), jnp.float32)], axis=0)
                columns.append(stack.astype(jnp.bfloat16))
        cols = jnp.concatenate(columns, axis=1)
        expo = jnp.dot(lhs[...], cols, preferred_element_type=jnp.float32)
        flux = jnp.sum(jnp.exp2(expo).reshape(gpoints, 8, cols.shape[1]), axis=0)
        for l in range(levels):
            parts = []
            for g in range(half // 8):
                at = 128 * (g * (levels + 1) + l)
                parts.append(flux[:, at : at + 128] - flux[:, at + 128 : at + 256])
            diff = jnp.concatenate(parts, axis=0)
            lit = jnp.broadcast_to(route[pl.ds(start_row, half), :], (half, 128)) < NDARK
            rate = diff / jnp.full((half, 128), mass[levels * me + l])
            heating[l, pl.ds(start_row, half), :] = jnp.where(lit, rate, 0.0)

    radiate(mine, prefix)
    to_rest.wait_recv()
    radiate(other, rest)

    for item in remap:
        wait_recv(item)
    for kl in range(levels):
        k = levels * me + kl
        weights = []
        for o in range(-RIM, RIM + 1):
            w = jnp.float32(0)
            for j in range(ridx.shape[1]):
                w = w + jnp.where(ridx[k, j] == k + o, rweight[k, j], jnp.float32(0))
            weights.append(w)
        for c in range(3):
            acc = weights[0] * ext[c, kl]
            for o in range(1, 2 * RIM + 1):
                acc = acc + weights[o] * ext[c, kl + o]
            new_state[c, kl] = acc

    for item in halo + to_chips + remap:
        wait_send(item)
    to_sib.wait_send()
    to_rest.wait_send()


def shards(state, coefs, lagged_absorbers, sun_route, band_coef, solar, layer_mass, remap_index, remap_weight):
    sizes = tuple(lax.axis_size(a) for a in ("grp", "gx", "gy"))
    chips = sizes[0] // 2
    gases = lagged_absorbers.shape[0]
    levels, rows = state.shape[1:3]
    vm = lambda: pl.BlockSpec(memory_space=pltpu.VMEM)
    sm = lambda: pl.BlockSpec(memory_space=pltpu.SMEM)
    hbm = lambda: pl.BlockSpec(memory_space=pl.ANY)
    f32, bf16 = jnp.float32, jnp.bfloat16
    n_copies = 8 + 1 + (chips - 1) + 1 + 2
    return pl.pallas_call(
        functools.partial(kernel, sizes),
        out_shape=(jax.ShapeDtypeStruct(state.shape, f32), jax.ShapeDtypeStruct(state.shape[1:], f32)),
        in_specs=[hbm(), hbm(), hbm(), vm(), vm(), vm(), sm(), sm(), sm()],
        out_specs=(vm(), vm()),
        scratch_shapes=[
            pltpu.VMEM((5, levels, rows + 2 * H, 128), f32),
            pltpu.VMEM(lagged_absorbers.shape, bf16),
            pltpu.VMEM((3, rows, 128), f32),
            pltpu.VMEM((3, rows, 128), f32),
            pltpu.VMEM((3, rows + 2 * H, 128), f32),
            pltpu.VMEM((3, rows + 2 * H, 128), f32),
            pltpu.VMEM((3, levels + 2 * RIM, rows, 128), f32),
            pltpu.VMEM((gases, rows, 128), f32),
            pltpu.VMEM((gases, rows // 2, 128), f32),
            pltpu.VMEM((gases, rows // 2, 128), f32),
            pltpu.VMEM((chips - 1, gases, rows // 2, 128), f32),
            pltpu.VMEM((gases, rows // 2, 128), f32),
            pltpu.VMEM((gases, rows // 2, 128), f32),
            pltpu.VMEM((gases, rows // 2, 128), f32),
            pltpu.VMEM((8 * band_coef.shape[0], 128), bf16),
            pltpu.SemaphoreType.DMA((3,)),
            pltpu.SemaphoreType.DMA((n_copies,)),
            pltpu.SemaphoreType.DMA((n_copies,)),
        ],
        compiler_params=pltpu.CompilerParams(collective_id=0, has_side_effects=True, vmem_limit_bytes=40 * 2**20),
    )(
        state, coefs, lagged_absorbers, sun_route, band_coef, solar.reshape(1, -1), layer_mass, remap_index, remap_weight,
    )


def solution(mesh):
    tiles = P(None, "grp", "gy", "gx")
    in_specs = (tiles, tiles, tiles, P("gy", "gx"), P(), P(), P(), P(), P())
    out_specs = (tiles, P("grp", "gy", "gx"))
    return jax.shard_map(shards, mesh=mesh, in_specs=in_specs, out_specs=out_specs, check_vma=False)
```

```python
import functools

import jax
import jax.numpy as jnp
from jax import lax
from jax.experimental import pallas as pl
from jax.experimental.pallas import tpu as pltpu
from jax.sharding import PartitionSpec as P

SUB = 8
RIM = 2
H = 2 * SUB
NDARK = 16
MESH = pl.DeviceIdType.MESH
LOG2E = 1.4426950408889634


def encode(values, biggest):
    return jnp.round(values * (32700.0 * jnp.exp2(-biggest))).astype(jnp.int32).astype(jnp.int16)


def decode(codes, biggest):
    return codes.astype(jnp.int32).astype(jnp.float32) * (jnp.exp2(biggest) * (1.0 / 32700.0))


def exponent(values):
    top = jnp.max(jnp.abs(values), axis=0, keepdims=True)
    return jnp.ceil(jnp.log2(jnp.maximum(top, 1e-30)) + 1e-3)


def lane_ids(rows):
    return lax.broadcasted_iota(jnp.int32, (rows, 128), 1)


def turned(v, shift):
    lane = lax.broadcasted_iota(jnp.int32, v.shape, 2)
    same = pltpu.roll(v, shift % 128, 2)
    across = pltpu.roll(same, 4, 1)
    keep = lane >= shift if shift > 0 else lane < 128 + shift
    return jnp.where(keep, same, across)


def chunks(start, stop, size=8):
    return [(i, min(i + size, stop)) for i in range(start, stop, size)]


def substeps(wide, p, fx, fy, bx, by, st, out):
    rows = wide.shape[1] // 8

    def row(c, r):
        return wide[c, pl.ds(r, 8, stride=rows), :]

    for i, j in chunks(0, rows):
        for r in range(i, j):
            p[r] = row(2, r)
            st[r] = row(4, r)
            fy[r] = row(1, r)
            by[r] = row(3, r)
            if r > 0:
                fx[r - 1] = row(0, r)
                bx[r - 1] = by[r]
        fy[i:j] = turned(fy[i:j], -1)
        by[i:j] = turned(by[i:j], -1)
    for step in range(SUB):
        low, high = 2 * step, rows - 2 * step
        for i, j in chunks(low, high - 2):
            here = p[i:j]
            new_x = fx[i:j] - bx[i:j] * (p[i + 2 : j + 2] - here)
            fx[i:j] = new_x
            k = max(i, low + 2)
            if k >= j:
                continue
            here = p[k:j]
            new_y = fy[k:j] - by[k:j] * (turned(here, -2) - here)
            fy[k:j] = new_y
            across = new_y - turned(new_y, 2)
            p[k:j] = here - st[k:j] * ((fx[k:j] - fx[k - 2 : j - 2]) + across)
    own = rows - 2 * H
    for i, j in chunks(0, own):
        moved = turned(fy[H + i : H + j], 1)
        for r in range(i, j):
            out[0, pl.ds(r, 8, stride=own), :] = fx[H + r - 1]
            out[1, pl.ds(r, 8, stride=own), :] = moved[r - i]
            out[2, pl.ds(r, 8, stride=own), :] = p[H + r]


def kernel(
    sizes,
    state, coefs, absorbers, route_row, band_rows, solar_row, mass_row, ridx_rows, rweight_rows,
    new_state, heating,
    route, band, solar, mass, ridx, rweight,
    wide, gas, rows_out, rows_in, sides_out, sides_in, corners_out, corners_in, exps, out, near,
    p, fx, fy, bx, by, st, block_sum, sib, chip_sum, lower, part, rest, prefix, lhs, sunlit,
    tile_sem, in_sem, send_sem, recv_sem,
):
    n_grp, n_gx, n_gy = sizes
    dyn_groups = 3 * n_grp // 4
    chips = n_grp // 2
    levels, rows = 4, 32
    me, gx, gy = lax.axis_index("grp"), lax.axis_index("gx"), lax.axis_index("gy")
    core, chip = lax.rem(me, 2), lax.div(me, 2)
    dyn = me < dyn_groups
    has_l, has_r = gx > 0, gx < n_gx - 1
    has_u, has_d = gy > 0, gy < n_gy - 1
    land = jnp.logical_and

    loads = [
        pltpu.make_async_copy(absorbers, gas, in_sem.at[0]),
        pltpu.make_async_copy(band_rows, band, in_sem.at[1]),
        pltpu.make_async_copy(solar_row, solar, in_sem.at[2]),
        pltpu.make_async_copy(route_row, route, in_sem.at[3]),
        pltpu.make_async_copy(ridx_rows, ridx, in_sem.at[4]),
        pltpu.make_async_copy(rweight_rows, rweight, in_sem.at[5]),
        pltpu.make_async_copy(mass_row, mass, in_sem.at[6]),
    ]
    tall_rows = rows + 2 * H
    tiles = []
    for l in range(levels):
        at = tall_rows * l + H
        tiles.append(pltpu.make_async_copy(state.at[:, l], wide.at[0:3, at : at + rows, :], tile_sem.at[0, l]))
        tiles.append(pltpu.make_async_copy(coefs.at[:, l], wide.at[3:5, at : at + rows, :], tile_sem.at[1, l]))
    for load in tiles + loads:
        load.start()

    partners = []
    for dx, cx in ((-1, has_l), (0, None), (1, has_r)):
        for dy, cy in ((-1, has_u), (0, None), (1, has_d)):
            if dx == 0 and dy == 0:
                continue
            cond = dyn
            if cx is not None:
                cond = land(cond, cx)
            if cy is not None:
                cond = land(cond, cy)
            partners.append((cond, {"gx": gx + dx, "gy": gy + dy}))
    steps = sorted({1} | {2 * d for d in range(1, chips)})
    for d in steps:
        partners.append((me + d < n_grp, {"grp": me + d}))
        partners.append((me - d >= 0, {"grp": me - d}))
    barrier = pltpu.get_barrier_semaphore()
    count = jnp.int32(0)
    for cond, dev in partners:
        count = count + cond.astype(jnp.int32)

        @pl.when(cond)
        def _(dev=dev):
            pl.semaphore_signal(barrier, inc=1, device_id=dev, device_id_type=MESH)

    number = [0]

    def remote(src, dst, dev):
        i = number[0]
        number[0] += 1
        return pltpu.make_async_remote_copy(
            src_ref=src, dst_ref=dst, send_sem=send_sem.at[i], recv_sem=recv_sem.at[i], device_id=dev, device_id_type=MESH
        )

    def all_of(*conds):
        return functools.reduce(land, conds)

    halo = [
        (all_of(dyn, has_d), all_of(dyn, has_u), remote(rows_out.at[:, rows - H :], rows_in.at[0], {"gy": gy + 1})),
        (all_of(dyn, has_u), all_of(dyn, has_d), remote(rows_out.at[:, 0:H], rows_in.at[1], {"gy": gy - 1})),
        (all_of(dyn, has_r), all_of(dyn, has_l), remote(sides_out.at[0], sides_in.at[0], {"gx": gx + 1})),
        (all_of(dyn, has_l), all_of(dyn, has_r), remote(sides_out.at[1], sides_in.at[1], {"gx": gx - 1})),
    ]
    for side, (to, back, dx) in enumerate(((has_r, has_l, 1), (has_l, has_r, -1))):
        bottom = corners_out.at[side, :, rows - H :]
        top = corners_out.at[side, :, 0:H]
        halo += [
            (all_of(dyn, to, has_d), all_of(dyn, back, has_u), remote(bottom, corners_in.at[side, 0], {"gx": gx + dx, "gy": gy + 1})),
            (all_of(dyn, to, has_u), all_of(dyn, back, has_d), remote(top, corners_in.at[side, 1], {"gx": gx + dx, "gy": gy - 1})),
        ]
    half = rows // 2
    mine = pl.multiple_of(half * core, half)
    other = pl.multiple_of(half * (1 - core), half)
    sibling = {"grp": me + 1 - 2 * core}
    to_sib = remote(block_sum.at[:, pl.ds(other, half)], sib, sibling)
    to_chips = [
        (chip + d < chips, chip - d >= 0, remote(chip_sum, lower.at[d - 1], {"grp": me + 2 * d})) for d in range(1, chips)
    ]
    to_rest = remote(part, rest, sibling)
    remap = [
        (me > 0, me < n_grp - 1, remote(out.at[:, 0 : RIM * rows], near.at[1], {"grp": me - 1})),
        (me < n_grp - 1, me > 0, remote(out.at[:, (levels - RIM) * rows : levels * rows], near.at[0], {"grp": me + 1})),
    ]

    def start(item):
        @pl.when(item[0])
        def _():
            item[2].start()

    def wait_recv(item):
        @pl.when(item[1])
        def _():
            item[2].wait_recv()

    def wait_send(item):
        @pl.when(item[0])
        def _():
            item[2].wait_send()

    for load in tiles:
        load.wait()

    lane = lane_ids(rows)
    exps[...] = jnp.zeros(exps.shape, jnp.float32)
    for q in range(3):
        right = jnp.zeros((rows, 128), jnp.float32)
        left = jnp.zeros((rows, 128), jnp.float32)
        for c in (2 * q, 2 * q + 1):
            if c > 4:
                continue
            for l in range(levels):
                t = 2 * l + c % 2
                cells = wide[c, tall_rows * l + H : tall_rows * l + H + rows, :]
                biggest = exponent(cells)
                exps[levels * c + l : levels * c + l + 1, :] = biggest
                rows_out[levels * c + l] = encode(cells, biggest)
                here = lax.div(lane, 16) == t
                shift = (16 * t + 16) % 128
                right = jnp.where(here, pltpu.roll(cells, shift, 1) if shift else cells, right)
                shift = 16 * t
                left = jnp.where(here, pltpu.roll(cells, shift, 1) if shift else cells, left)
        for side, strip in enumerate((right, left)):
            biggest = exponent(strip)
            sides_out[side, q, 0:rows] = encode(strip, biggest)
            sides_out[side, q, rows : rows + 16] = jnp.broadcast_to(biggest, (16, 128)).astype(jnp.int32).astype(jnp.int16)
            corners_out[side, q] = strip.astype(jnp.bfloat16)
    for i in range(2):
        held = exps[16 * i : 16 * i + 16, :]
        rows_out[20 + i] = jnp.concatenate([held, held], axis=0).astype(jnp.int32).astype(jnp.int16)

    pl.semaphore_wait(barrier, count)
    for item in halo:
        start(item)

    loads[0].wait()
    for f in range(gas.shape[0]):
        total = gas[f, 0].astype(jnp.float32)
        for l in range(1, levels):
            total = total + gas[f, l].astype(jnp.float32)
        block_sum[f] = total
    to_sib.start()

    def fill(cond, ref, *index, value=0):
        @pl.when(cond)
        def _():
            view = ref.at[index] if index else ref
            view[...] = jnp.full(view.shape, value, view.dtype)

    fill(~has_u, rows_in, 0)
    fill(~has_d, rows_in, 1)
    fill(~has_l, sides_in, 0)
    fill(~has_r, sides_in, 1)
    fill(~land(has_l, has_u), corners_in, 0, 0)
    fill(~land(has_l, has_d), corners_in, 0, 1)
    fill(~land(has_r, has_u), corners_in, 1, 0)
    fill(~land(has_r, has_d), corners_in, 1, 1)
    fill(me == 0, near, 0)
    fill(me == n_grp - 1, near, 1)
    for d in range(1, chips):
        fill(chip - d < 0, lower, d - 1, value=-4 * 8191)

    @pl.when(~dyn)
    def _():
        for c in range(3):
            for l in range(levels):
                out[c, rows * l : rows * l + rows, :] = wide[c, tall_rows * l + H : tall_rows * l + H + rows, :]

    for load in loads[1:]:
        load.wait()
    gases, gpoints = band.shape
    r0 = lax.broadcasted_iota(jnp.int32, (gpoints, gpoints), 0)
    r1 = lax.broadcasted_iota(jnp.int32, (gpoints, gpoints), 1)
    logs = jnp.log2(solar[...])
    high = logs.astype(jnp.bfloat16).astype(jnp.float32)
    middle = (logs - high).astype(jnp.bfloat16).astype(jnp.float32)
    low = logs - high - middle
    srcs = jnp.concatenate([band[...].astype(jnp.float32), high, middle, low], axis=0).astype(jnp.bfloat16)
    n_src = gases + 3
    l0 = lax.broadcasted_iota(jnp.int32, (rows, rows), 0)
    l1 = lax.broadcasted_iota(jnp.int32, (rows, rows), 1)
    lit_row = jnp.broadcast_to((route[...] < NDARK).astype(jnp.float32), (rows, rows))
    sunlit[...] = jnp.broadcast_to(jnp.sum(jnp.where(l0 == l1, lit_row, 0.0), axis=1, keepdims=True), (rows, 128))
    spread0 = lax.div(lax.broadcasted_iota(jnp.int32, (8 * gpoints, gpoints), 0), 8)
    spread1 = lax.broadcasted_iota(jnp.int32, (8 * gpoints, gpoints), 1)
    spread = (spread0 == spread1).astype(jnp.float32).astype(jnp.bfloat16)
    tall = lax.dot_general(spread, srcs, (((1,), (1,)), ((), ())), preferred_element_type=jnp.float32).astype(jnp.bfloat16)
    w0 = lax.broadcasted_iota(jnp.int32, (n_src, 128), 0)
    w1 = lax.broadcasted_iota(jnp.int32, (n_src, 128), 1)
    in_gas = w1 < 16 * gases
    owner = jnp.where(in_gas, lax.rem(lax.div(w1, 8), gases), w1 - 16 * gases + gases)
    widen = (w0 == owner).astype(jnp.float32).astype(jnp.bfloat16)
    spread_all = jnp.dot(tall, widen, preferred_element_type=jnp.float32)
    m0 = lax.broadcasted_iota(jnp.int32, (8 * gpoints, 128), 0)
    m1 = lax.broadcasted_iota(jnp.int32, (8 * gpoints, 128), 1)
    keep = (m1 >= 16 * gases) | (lax.rem(m0, 8) == lax.rem(m1, 8))
    lhs[...] = jnp.where(keep, spread_all, 0.0).astype(jnp.bfloat16)

    to_sib.wait_recv()
    both = block_sum[:, pl.ds(mine, half), :] + sib[...]
    chip_sum[...] = jnp.round((both - 4.0) * 8191.0).astype(jnp.int32).astype(jnp.int16)
    for item in to_chips:
        start(item)

    for item in halo:
        wait_recv(item)

    @pl.when(dyn)
    def _():
        for i, at in enumerate((0, H + rows)):
            biggest = jnp.concatenate([rows_in[i, 20], rows_in[i, 21]], axis=0).astype(jnp.int32).astype(jnp.float32)
            exps[...] = biggest
            for c in range(5):
                for l in range(levels):
                    k = levels * c + l
                    wide[c, tall_rows * l + at : tall_rows * l + at + H, :] = decode(rows_in[i, k], exps[k : k + 1, :])
        lane_w = lane_ids(rows + 2 * H)
        for q in range(3):
            strips = []
            for side in range(2):
                biggest = sides_in[side, q, rows : rows + 16].astype(jnp.int32).astype(jnp.float32)[0:1]
                middle = decode(sides_in[side, q, 0:rows], biggest)
                ends = [corners_in[side, i, q].astype(jnp.float32) for i in range(2)]
                strips.append(jnp.concatenate([ends[0], middle, ends[1]], axis=0))
            for c in (2 * q, 2 * q + 1):
                if c > 4:
                    continue
                for l in range(levels):
                    t = 2 * l + c % 2
                    shift = (112 - 16 * t) % 128
                    left = pltpu.roll(strips[0], shift, 1) if shift else strips[0]
                    shift = (128 - 16 * t) % 128
                    right = pltpu.roll(strips[1], shift, 1) if shift else strips[1]
                    wide[c, tall_rows * (levels + l) : tall_rows * (levels + l + 1), :] = jnp.where(
                        lane_w < 16, right, jnp.where(lane_w >= 112, left, 0.0)
                    )
        substeps(wide, p, fx, fy, bx, by, st, out)

    for item in remap:
        start(item)

    for item in to_chips:
        wait_recv(item)
    above = jnp.zeros(rest.shape, jnp.float32)
    for d in range(1, chips):
        above = above + (lower[d - 1].astype(jnp.int32).astype(jnp.float32) * (1.0 / 8191.0) + 4.0)
    even = (core == 0).astype(jnp.float32)
    part[...] = above + even * block_sum[:, pl.ds(mine, half), :]
    to_rest.start()
    prefix[...] = above + (1.0 - even) * sib[...]

    def radiate(start_row, ref):
        columns = []
        for g in range(half // 8):
            depth = ref[:, 8 * g : 8 * g + 8, :]
            for l in range(levels + 1):
                if l:
                    cells = gas[:, l - 1, pl.ds(start_row, half), :].astype(jnp.float32)
                    depth = depth + cells[:, 8 * g : 8 * g + 8, :]
                scaled = (depth * -LOG2E).reshape(8 * gases, 128)
                high = scaled.astype(jnp.bfloat16).astype(jnp.float32)
                stack = jnp.concatenate([high, scaled - high, jnp.ones((128 - 16 * gases, 128), jnp.float32)], axis=0)
                columns.append(stack.astype(jnp.bfloat16))
        cols = jnp.concatenate(columns, axis=1)
        expo = jnp.dot(lhs[...], cols, preferred_element_type=jnp.float32)
        flux = jnp.sum(jnp.exp2(expo).reshape(gpoints, 8, cols.shape[1]), axis=0)
        for l in range(levels):
            parts = []
            for g in range(half // 8):
                at = 128 * (g * (levels + 1) + l)
                parts.append(flux[:, at : at + 128] - flux[:, at + 128 : at + 256])
            diff = jnp.concatenate(parts, axis=0)
            lit = sunlit[pl.ds(start_row, half), :] > 0.5
            rate = diff / jnp.full((half, 128), mass[0, levels * me + l])
            heating[l, pl.ds(start_row, half), :] = jnp.where(lit, rate, 0.0)

    radiate(mine, prefix)
    to_rest.wait_recv()
    radiate(other, rest)

    for item in remap:
        wait_recv(item)
    for kl in range(levels):
        k = levels * me + kl
        weights = []
        for o in range(-RIM, RIM + 1):
            w = jnp.float32(0)
            for j in range(ridx.shape[0]):
                w = w + jnp.where(ridx[j, k] == k + o, rweight[j, k], jnp.float32(0))
            weights.append(w)
        for c in range(3):
            acc = jnp.zeros((rows, 128), jnp.float32)
            for o in range(-RIM, RIM + 1):
                m = kl + o
                ref, m = (near.at[0], m + RIM) if m < 0 else (out, m) if m < levels else (near.at[1], m - levels)
                cells = ref[c, rows * m : rows * m + rows, :]
                acc = acc + weights[o + RIM] * cells
            new_state[c, kl] = acc

    for item in halo + to_chips + remap:
        wait_send(item)
    to_sib.wait_send()
    to_rest.wait_send()


def shards(state, coefs, lagged_absorbers, sun_route, band_coef, solar, layer_mass, remap_index, remap_weight):
    sizes = tuple(lax.axis_size(a) for a in ("grp", "gx", "gy"))
    chips = sizes[0] // 2
    gases = lagged_absorbers.shape[0]
    levels, rows = state.shape[1:3]
    f32, bf16, i16 = jnp.float32, jnp.bfloat16, jnp.int16
    operands = (
        state, coefs, lagged_absorbers, sun_route.T, band_coef.T, solar.reshape(1, -1), layer_mass.reshape(1, -1),
        remap_index.T, remap_weight.T,
    )
    n_copies = 8 + 1 + (chips - 1) + 1 + 2
    return pl.pallas_call(
        functools.partial(kernel, sizes),
        out_shape=(jax.ShapeDtypeStruct(state.shape, f32), jax.ShapeDtypeStruct(state.shape[1:], f32)),
        in_specs=[pl.BlockSpec(memory_space=pltpu.HBM)] * len(operands),
        out_specs=(pl.BlockSpec(memory_space=pltpu.VMEM),) * 2,
        scratch_shapes=[
            pltpu.VMEM((1, rows), jnp.int32),
            pltpu.VMEM(band_coef.shape[::-1], bf16),
            pltpu.VMEM((1, solar.shape[0]), f32),
            pltpu.SMEM((1, layer_mass.shape[0]), f32),
            pltpu.SMEM(remap_index.shape[::-1], jnp.int32),
            pltpu.SMEM(remap_weight.shape[::-1], f32),
            pltpu.VMEM((5, 2 * levels * (rows + 2 * H), 128), f32),
            pltpu.VMEM(lagged_absorbers.shape, bf16),
            pltpu.VMEM((22, rows, 128), i16),
            pltpu.VMEM((2, 22, H, 128), i16),
            pltpu.VMEM((2, 3, rows + 16, 128), i16),
            pltpu.VMEM((2, 3, rows + 16, 128), i16),
            pltpu.VMEM((2, 3, rows, 128), bf16),
            pltpu.VMEM((2, 2, 3, H, 128), bf16),
            pltpu.VMEM((32, 128), f32),
            pltpu.VMEM((3, 2 * levels * rows, 128), f32),
            pltpu.VMEM((2, 3, RIM * rows, 128), f32),
            *[pltpu.VMEM((rows + 2 * H, 2 * levels, 128), f32)] * 6,
            pltpu.VMEM((gases, rows, 128), f32),
            pltpu.VMEM((gases, rows // 2, 128), f32),
            pltpu.VMEM((gases, rows // 2, 128), i16),
            pltpu.VMEM((chips - 1, gases, rows // 2, 128), i16),
            pltpu.VMEM((gases, rows // 2, 128), f32),
            pltpu.VMEM((gases, rows // 2, 128), f32),
            pltpu.VMEM((gases, rows // 2, 128), f32),
            pltpu.VMEM((8 * band_coef.shape[0], 128), bf16),
            pltpu.VMEM((rows, 128), f32),
            pltpu.SemaphoreType.DMA((2, levels)),
            pltpu.SemaphoreType.DMA((7,)),
            pltpu.SemaphoreType.DMA((n_copies,)),
            pltpu.SemaphoreType.DMA((n_copies,)),
        ],
        compiler_params=pltpu.CompilerParams(collective_id=0, has_side_effects=True, vmem_limit_bytes=40 * 2**20),
    )(
        *[pltpu.with_memory_space_constraint(a, pltpu.HBM) for a in operands]
    )


def solution(mesh):
    tiles = P(None, "grp", "gy", "gx")
    in_specs = (tiles, tiles, tiles, P("gy", "gx"), P(), P(), P(), P(), P())
    out_specs = (tiles, P("grp", "gy", "gx"))
    return jax.shard_map(shards, mesh=mesh, in_specs=in_specs, out_specs=out_specs, check_vma=False)
```

```python
import functools

import jax
import jax.numpy as jnp
from jax import lax
from jax.experimental import pallas as pl
from jax.experimental.pallas import tpu as pltpu
from jax.sharding import PartitionSpec as P

SUB = 8
RIM = 2
H = 2 * SUB
NDARK = 16
PLANES = 22
DIRECT = 14
MESH = pl.DeviceIdType.MESH
LOG2E = 1.4426950408889634


def encode(values, biggest):
    return jnp.round(values * (32700.0 * jnp.exp2(-biggest))).astype(jnp.int32).astype(jnp.int16)


def decode(codes, biggest):
    return codes.astype(jnp.int32).astype(jnp.float32) * (jnp.exp2(biggest) * (1.0 / 32700.0))


def exponent(values):
    top = jnp.max(jnp.abs(values), axis=0, keepdims=True)
    return jnp.ceil(jnp.log2(jnp.maximum(top, 1e-30)) + 1e-3)


def lane_ids(rows):
    return lax.broadcasted_iota(jnp.int32, (rows, 128), 1)


def turned(v, shift):
    lane = lax.broadcasted_iota(jnp.int32, v.shape, 2)
    same = pltpu.roll(v, shift % 128, 2)
    across = pltpu.roll(same, 4, 1)
    keep = lane >= shift if shift > 0 else lane < 128 + shift
    return jnp.where(keep, same, across)


def chunks(start, stop, size=8):
    return [(i, min(i + size, stop)) for i in range(start, stop, size)]


def substeps(wide, p, fx, fy, bx, by, st, out):
    rows = wide.shape[1] // 8

    def row(c, r):
        return wide[c, pl.ds(r, 8, stride=rows), :]

    for i, j in chunks(0, rows):
        for r in range(i, j):
            p[r] = row(2, r)
            st[r] = row(4, r)
            fy[r] = row(1, r)
            by[r] = row(3, r)
            if r > 0:
                fx[r - 1] = row(0, r)
                bx[r - 1] = by[r]
        fy[i:j] = turned(fy[i:j], -1)
        by[i:j] = turned(by[i:j], -1)
    first = 0
    pv, xv, yv = p[...], fx[0 : rows - 1], fy[...]
    for step in range(SUB):
        n = rows - 2 * first
        xv = xv[0 : n - 2] - bx[first : first + n - 2] * (pv[2:n] - pv[0 : n - 2])
        here = pv[2 : n - 2]
        inner = slice(first + 2, first + n - 2)
        yv = yv[2 : n - 2] - by[inner] * (turned(here, -2) - here)
        across = yv - turned(yv, 2)
        pv = here - st[inner] * ((xv[2 : n - 2] - xv[0 : n - 4]) + across)
        last, xv = xv, xv[2 : n - 2]
        first += 2
    own = rows - 2 * H
    moved = turned(yv, 1)
    for r in range(own):
        out[0, pl.ds(r, 8, stride=own), :] = last[r + 1]
        out[1, pl.ds(r, 8, stride=own), :] = moved[r]
        out[2, pl.ds(r, 8, stride=own), :] = pv[r]


def kernel(
    sizes,
    state, coefs, absorbers, route_row, band_rows, solar_row, mass_row, ridx_rows, rweight_rows,
    new_state, heating,
    route, band, solar, mass, ridx, rweight,
    wide, gas, rows_out, rows_in, sides_out, sides_in, corners_out, corners_in, exps, out, near, passing,
    p, fx, fy, bx, by, st, block_sum, sib, chip_sum, lower, part, rest, prefix, lhs, sunlit,
    tile_sem, in_sem, send_sem, recv_sem,
):
    n_grp, n_gx, n_gy = sizes
    dyn_groups = 3 * n_grp // 4
    chips = n_grp // 2
    levels, rows = 4, 32
    me, gx, gy = lax.axis_index("grp"), lax.axis_index("gx"), lax.axis_index("gy")
    core, chip = lax.rem(me, 2), lax.div(me, 2)
    dyn = me < dyn_groups
    has_l, has_r = gx > 0, gx < n_gx - 1
    has_u, has_d = gy > 0, gy < n_gy - 1
    land = jnp.logical_and

    loads = [
        pltpu.make_async_copy(absorbers, gas, in_sem.at[0]),
        pltpu.make_async_copy(band_rows, band, in_sem.at[1]),
        pltpu.make_async_copy(solar_row, solar, in_sem.at[2]),
        pltpu.make_async_copy(route_row, route, in_sem.at[3]),
        pltpu.make_async_copy(ridx_rows, ridx, in_sem.at[4]),
        pltpu.make_async_copy(rweight_rows, rweight, in_sem.at[5]),
        pltpu.make_async_copy(mass_row, mass, in_sem.at[6]),
    ]
    tall_rows = rows + 2 * H
    tiles = []
    for l in range(levels):
        at = tall_rows * l + H
        tiles.append(pltpu.make_async_copy(state.at[:, l], wide.at[0:3, at : at + rows, :], tile_sem.at[0, l]))
        tiles.append(pltpu.make_async_copy(coefs.at[:, l], wide.at[3:5, at : at + rows, :], tile_sem.at[1, l]))
    for load in tiles + loads:
        load.start()

    partners = []
    for dx, cx in ((-1, has_l), (0, None), (1, has_r)):
        for dy, cy in ((-1, has_u), (0, None), (1, has_d)):
            if dx == 0 and dy == 0:
                continue
            cond = dyn
            if cx is not None:
                cond = land(cond, cx)
            if cy is not None:
                cond = land(cond, cy)
            partners.append((cond, {"gx": gx + dx, "gy": gy + dy}))
    seam = n_gy // 2
    far = seam >= 2
    edge_d, edge_u = land(dyn, gy == seam - 1), land(dyn, gy == seam)
    pass_d, pass_u = land(dyn, gy == seam - 2), land(dyn, gy == seam + 1)
    if far:
        partners += [(pass_d, {"gy": gy + 2}), (edge_u, {"gy": gy - 2}), (pass_u, {"gy": gy - 2}), (edge_d, {"gy": gy + 2})]
    steps = sorted({1} | {2 * d for d in range(1, chips)})
    for d in steps:
        partners.append((me + d < n_grp, {"grp": me + d}))
        partners.append((me - d >= 0, {"grp": me - d}))
    barrier = pltpu.get_barrier_semaphore()
    count = jnp.int32(0)
    for cond, dev in partners:
        count = count + cond.astype(jnp.int32)

        @pl.when(cond)
        def _(dev=dev):
            pl.semaphore_signal(barrier, inc=1, device_id=dev, device_id_type=MESH)

    number = [0]

    def remote(src, dst, dev, arrival=None):
        i = number[0]
        number[0] += 1
        return pltpu.make_async_remote_copy(
            src_ref=src,
            dst_ref=dst,
            send_sem=send_sem.at[i],
            recv_sem=recv_sem.at[i if arrival is None else arrival],
            device_id=dev,
            device_id_type=MESH,
        )

    def all_of(*conds):
        return functools.reduce(land, conds)

    down, up = all_of(dyn, has_d), all_of(dyn, has_u)
    halo = [
        (down, up, remote(rows_out.at[0:DIRECT, rows - H :], rows_in.at[0, 0:DIRECT], {"gy": gy + 1})),
        (up, down, remote(rows_out.at[0:DIRECT, 0:H], rows_in.at[1, 0:DIRECT], {"gy": gy - 1})),
    ]
    rest_down = rows_out.at[DIRECT:PLANES, rows - H :]
    rest_up = rows_out.at[DIRECT:PLANES, 0:H]
    down_sem, up_sem, pass_sem = number[0], number[0] + 1, number[0] + 2
    by_down = (land(down, ~edge_d) if far else down, up, remote(rest_down, rows_in.at[0, DIRECT:PLANES], {"gy": gy + 1}))
    by_up = (land(up, ~edge_u) if far else up, down, remote(rest_up, rows_in.at[1, DIRECT:PLANES], {"gy": gy - 1}))
    passes = []
    if far:
        to_pass_d = (edge_d, pass_d, remote(rest_down, passing, {"gy": gy - 1}))
        to_pass_u = (edge_u, pass_u, remote(rest_up, passing, {"gy": gy + 1}, pass_sem))
        passes = [to_pass_d, to_pass_u]
    relays = []
    if far:
        relays = [
            (pass_d, None, remote(passing, rows_in.at[0, DIRECT:PLANES], {"gy": gy + 2}, down_sem)),
            (pass_u, None, remote(passing, rows_in.at[1, DIRECT:PLANES], {"gy": gy - 2}, up_sem)),
        ]
    halo = halo + [by_down, by_up] + [
        (all_of(dyn, has_r), all_of(dyn, has_l), remote(sides_out.at[0], sides_in.at[0], {"gx": gx + 1})),
        (all_of(dyn, has_l), all_of(dyn, has_r), remote(sides_out.at[1], sides_in.at[1], {"gx": gx - 1})),
    ]
    for side, (to, back, dx) in enumerate(((has_r, has_l, 1), (has_l, has_r, -1))):
        bottom = corners_out.at[side, :, rows - H :]
        top = corners_out.at[side, :, 0:H]
        halo += [
            (all_of(dyn, to, has_d), all_of(dyn, back, has_u), remote(bottom, corners_in.at[side, 0], {"gx": gx + dx, "gy": gy + 1})),
            (all_of(dyn, to, has_u), all_of(dyn, back, has_d), remote(top, corners_in.at[side, 1], {"gx": gx + dx, "gy": gy - 1})),
        ]
    half = rows // 2
    mine = pl.multiple_of(half * core, half)
    other = pl.multiple_of(half * (1 - core), half)
    sibling = {"grp": me + 1 - 2 * core}
    to_sib = remote(block_sum.at[:, pl.ds(other, half)], sib, sibling)
    to_chips = [
        (chip + d < chips, chip - d >= 0, remote(chip_sum, lower.at[d - 1], {"grp": me + 2 * d})) for d in range(1, chips)
    ]
    to_rest = remote(part, rest, sibling)
    remap = [
        (me > 0, me < n_grp - 1, remote(out.at[:, 0 : RIM * rows], near.at[1], {"grp": me - 1})),
        (me < n_grp - 1, me > 0, remote(out.at[:, (levels - RIM) * rows : levels * rows], near.at[0], {"grp": me + 1})),
    ]

    def start(item):
        @pl.when(item[0])
        def _():
            item[2].start()

    def wait_recv(item):
        @pl.when(item[1])
        def _():
            item[2].wait_recv()

    def wait_send(item):
        @pl.when(item[0])
        def _():
            item[2].wait_send()

    for load in tiles:
        load.wait()

    lane = lane_ids(rows)
    exps[...] = jnp.zeros(exps.shape, jnp.float32)
    for q in range(3):
        right = jnp.zeros((rows, 128), jnp.float32)
        left = jnp.zeros((rows, 128), jnp.float32)
        for c in (2 * q, 2 * q + 1):
            if c > 4:
                continue
            for l in range(levels):
                t = 2 * l + c % 2
                cells = wide[c, tall_rows * l + H : tall_rows * l + H + rows, :]
                biggest = exponent(cells)
                exps[levels * c + l : levels * c + l + 1, :] = biggest
                rows_out[levels * c + l] = encode(cells, biggest)
                here = lax.div(lane, 16) == t
                shift = (16 * t + 16) % 128
                right = jnp.where(here, pltpu.roll(cells, shift, 1) if shift else cells, right)
                shift = 16 * t
                left = jnp.where(here, pltpu.roll(cells, shift, 1) if shift else cells, left)
        for side, strip in enumerate((right, left)):
            biggest = exponent(strip)
            sides_out[side, q, 0:rows] = encode(strip, biggest)
            sides_out[side, q, rows : rows + 16] = jnp.broadcast_to(biggest, (16, 128)).astype(jnp.int32).astype(jnp.int16)
            corners_out[side, q] = strip.astype(jnp.bfloat16)
    for i in range(2):
        held = exps[16 * i : 16 * i + 16, :]
        rows_out[20 + i] = jnp.concatenate([held, held], axis=0).astype(jnp.int32).astype(jnp.int16)

    pl.semaphore_wait(barrier, count)
    for item in passes + halo:
        start(item)

    loads[0].wait()
    for f in range(gas.shape[0]):
        total = gas[f, 0].astype(jnp.float32)
        for l in range(1, levels):
            total = total + gas[f, l].astype(jnp.float32)
        block_sum[f] = total
    to_sib.start()
    for item, relay in zip(passes, relays):
        wait_recv(item)
        start(relay)

    def fill(cond, ref, *index, value=0):
        @pl.when(cond)
        def _():
            view = ref.at[index] if index else ref
            view[...] = jnp.full(view.shape, value, view.dtype)

    fill(~has_u, rows_in, 0)
    fill(~has_d, rows_in, 1)
    fill(~has_l, sides_in, 0)
    fill(~has_r, sides_in, 1)
    fill(~land(has_l, has_u), corners_in, 0, 0)
    fill(~land(has_l, has_d), corners_in, 0, 1)
    fill(~land(has_r, has_u), corners_in, 1, 0)
    fill(~land(has_r, has_d), corners_in, 1, 1)
    fill(me == 0, near, 0)
    fill(me == n_grp - 1, near, 1)
    for d in range(1, chips):
        fill(chip - d < 0, lower, d - 1, value=-4 * 8191)

    @pl.when(~dyn)
    def _():
        for c in range(3):
            for l in range(levels):
                out[c, rows * l : rows * l + rows, :] = wide[c, tall_rows * l + H : tall_rows * l + H + rows, :]

    for load in loads[1:]:
        load.wait()
    gases, gpoints = band.shape
    r0 = lax.broadcasted_iota(jnp.int32, (gpoints, gpoints), 0)
    r1 = lax.broadcasted_iota(jnp.int32, (gpoints, gpoints), 1)
    logs = jnp.log2(solar[...])
    high = logs.astype(jnp.bfloat16).astype(jnp.float32)
    middle = (logs - high).astype(jnp.bfloat16).astype(jnp.float32)
    low = logs - high - middle
    srcs = jnp.concatenate([band[...].astype(jnp.float32), high, middle, low], axis=0).astype(jnp.bfloat16)
    n_src = gases + 3
    l0 = lax.broadcasted_iota(jnp.int32, (rows, rows), 0)
    l1 = lax.broadcasted_iota(jnp.int32, (rows, rows), 1)
    lit_row = jnp.broadcast_to((route[...] < NDARK).astype(jnp.float32), (rows, rows))
    sunlit[...] = jnp.broadcast_to(jnp.sum(jnp.where(l0 == l1, lit_row, 0.0), axis=1, keepdims=True), (rows, 128))
    spread0 = lax.div(lax.broadcasted_iota(jnp.int32, (8 * gpoints, gpoints), 0), 8)
    spread1 = lax.broadcasted_iota(jnp.int32, (8 * gpoints, gpoints), 1)
    spread = (spread0 == spread1).astype(jnp.float32).astype(jnp.bfloat16)
    tall = lax.dot_general(spread, srcs, (((1,), (1,)), ((), ())), preferred_element_type=jnp.float32).astype(jnp.bfloat16)
    w0 = lax.broadcasted_iota(jnp.int32, (n_src, 128), 0)
    w1 = lax.broadcasted_iota(jnp.int32, (n_src, 128), 1)
    in_gas = w1 < 16 * gases
    owner = jnp.where(in_gas, lax.rem(lax.div(w1, 8), gases), w1 - 16 * gases + gases)
    widen = (w0 == owner).astype(jnp.float32).astype(jnp.bfloat16)
    spread_all = jnp.dot(tall, widen, preferred_element_type=jnp.float32)
    m0 = lax.broadcasted_iota(jnp.int32, (8 * gpoints, 128), 0)
    m1 = lax.broadcasted_iota(jnp.int32, (8 * gpoints, 128), 1)
    keep = (m1 >= 16 * gases) | (lax.rem(m0, 8) == lax.rem(m1, 8))
    lhs[...] = jnp.where(keep, spread_all, 0.0).astype(jnp.bfloat16)

    to_sib.wait_recv()
    both = block_sum[:, pl.ds(mine, half), :] + sib[...]
    chip_sum[...] = jnp.round((both - 4.0) * 8191.0).astype(jnp.int32).astype(jnp.int16)
    for item in to_chips:
        start(item)

    for item in halo:
        wait_recv(item)

    @pl.when(dyn)
    def _():
        for i, at in enumerate((0, H + rows)):
            biggest = jnp.concatenate([rows_in[i, 20], rows_in[i, 21]], axis=0).astype(jnp.int32).astype(jnp.float32)
            exps[...] = biggest
            for c in range(5):
                for l in range(levels):
                    k = levels * c + l
                    wide[c, tall_rows * l + at : tall_rows * l + at + H, :] = decode(rows_in[i, k], exps[k : k + 1, :])
        lane_w = lane_ids(rows + 2 * H)
        for q in range(3):
            strips = []
            for side in range(2):
                biggest = sides_in[side, q, rows : rows + 16].astype(jnp.int32).astype(jnp.float32)[0:1]
                middle = decode(sides_in[side, q, 0:rows], biggest)
                ends = [corners_in[side, i, q].astype(jnp.float32) for i in range(2)]
                strips.append(jnp.concatenate([ends[0], middle, ends[1]], axis=0))
            for c in (2 * q, 2 * q + 1):
                if c > 4:
                    continue
                for l in range(levels):
                    t = 2 * l + c % 2
                    shift = (112 - 16 * t) % 128
                    left = pltpu.roll(strips[0], shift, 1) if shift else strips[0]
                    shift = (128 - 16 * t) % 128
                    right = pltpu.roll(strips[1], shift, 1) if shift else strips[1]
                    wide[c, tall_rows * (levels + l) : tall_rows * (levels + l + 1), :] = jnp.where(
                        lane_w < 16, right, jnp.where(lane_w >= 112, left, 0.0)
                    )
        substeps(wide, p, fx, fy, bx, by, st, out)

    for item in remap:
        start(item)

    for item in to_chips:
        wait_recv(item)
    above = jnp.zeros(rest.shape, jnp.float32)
    for d in range(1, chips):
        above = above + (lower[d - 1].astype(jnp.int32).astype(jnp.float32) * (1.0 / 8191.0) + 4.0)
    even = (core == 0).astype(jnp.float32)
    part[...] = above + even * block_sum[:, pl.ds(mine, half), :]
    to_rest.start()
    prefix[...] = above + (1.0 - even) * sib[...]

    def radiate(start_row, ref):
        columns = []
        for g in range(half // 8):
            depth = ref[:, 8 * g : 8 * g + 8, :]
            for l in range(levels + 1):
                if l:
                    cells = gas[:, l - 1, pl.ds(start_row, half), :].astype(jnp.float32)
                    depth = depth + cells[:, 8 * g : 8 * g + 8, :]
                scaled = (depth * -LOG2E).reshape(8 * gases, 128)
                high = scaled.astype(jnp.bfloat16).astype(jnp.float32)
                stack = jnp.concatenate([high, scaled - high, jnp.ones((128 - 16 * gases, 128), jnp.float32)], axis=0)
                columns.append(stack.astype(jnp.bfloat16))
        cols = jnp.concatenate(columns, axis=1)
        expo = jnp.dot(lhs[...], cols, preferred_element_type=jnp.float32)
        flux = jnp.sum(jnp.exp2(expo).reshape(gpoints, 8, cols.shape[1]), axis=0)
        for l in range(levels):
            parts = []
            for g in range(half // 8):
                at = 128 * (g * (levels + 1) + l)
                parts.append(flux[:, at : at + 128] - flux[:, at + 128 : at + 256])
            diff = jnp.concatenate(parts, axis=0)
            lit = sunlit[pl.ds(start_row, half), :] > 0.5
            rate = diff / jnp.full((half, 128), mass[0, levels * me + l])
            heating[l, pl.ds(start_row, half), :] = jnp.where(lit, rate, 0.0)

    radiate(mine, prefix)
    to_rest.wait_recv()
    radiate(other, rest)

    for item in remap:
        wait_recv(item)
    for kl in range(levels):
        k = levels * me + kl
        weights = []
        for o in range(-RIM, RIM + 1):
            w = jnp.float32(0)
            for j in range(ridx.shape[0]):
                w = w + jnp.where(ridx[j, k] == k + o, rweight[j, k], jnp.float32(0))
            weights.append(w)
        for c in range(3):
            acc = jnp.zeros((rows, 128), jnp.float32)
            for o in range(-RIM, RIM + 1):
                m = kl + o
                ref, m = (near.at[0], m + RIM) if m < 0 else (out, m) if m < levels else (near.at[1], m - levels)
                cells = ref[c, rows * m : rows * m + rows, :]
                acc = acc + weights[o + RIM] * cells
            new_state[c, kl] = acc

    for item in passes + relays + halo + to_chips + remap:
        wait_send(item)
    to_sib.wait_send()
    to_rest.wait_send()


def shards(state, coefs, lagged_absorbers, sun_route, band_coef, solar, layer_mass, remap_index, remap_weight):
    sizes = tuple(lax.axis_size(a) for a in ("grp", "gx", "gy"))
    chips = sizes[0] // 2
    gases = lagged_absorbers.shape[0]
    levels, rows = state.shape[1:3]
    f32, bf16, i16 = jnp.float32, jnp.bfloat16, jnp.int16
    operands = (
        state, coefs, lagged_absorbers, sun_route.T, band_coef.T, solar.reshape(1, -1), layer_mass.reshape(1, -1),
        remap_index.T, remap_weight.T,
    )
    n_copies = 14 + 1 + (chips - 1) + 1 + 2
    return pl.pallas_call(
        functools.partial(kernel, sizes),
        out_shape=(jax.ShapeDtypeStruct(state.shape, f32), jax.ShapeDtypeStruct(state.shape[1:], f32)),
        in_specs=[pl.BlockSpec(memory_space=pltpu.HBM)] * len(operands),
        out_specs=(pl.BlockSpec(memory_space=pltpu.VMEM),) * 2,
        scratch_shapes=[
            pltpu.VMEM((1, rows), jnp.int32),
            pltpu.VMEM(band_coef.shape[::-1], bf16),
            pltpu.VMEM((1, solar.shape[0]), f32),
            pltpu.SMEM((1, layer_mass.shape[0]), f32),
            pltpu.SMEM(remap_index.shape[::-1], jnp.int32),
            pltpu.SMEM(remap_weight.shape[::-1], f32),
            pltpu.VMEM((5, 2 * levels * (rows + 2 * H), 128), f32),
            pltpu.VMEM(lagged_absorbers.shape, bf16),
            pltpu.VMEM((PLANES, rows, 128), i16),
            pltpu.VMEM((2, PLANES, H, 128), i16),
            pltpu.VMEM((2, 3, rows + 16, 128), i16),
            pltpu.VMEM((2, 3, rows + 16, 128), i16),
            pltpu.VMEM((2, 3, rows, 128), bf16),
            pltpu.VMEM((2, 2, 3, H, 128), bf16),
            pltpu.VMEM((32, 128), f32),
            pltpu.VMEM((3, 2 * levels * rows, 128), f32),
            pltpu.VMEM((2, 3, RIM * rows, 128), f32),
            pltpu.VMEM((PLANES - DIRECT, H, 128), i16),
            *[pltpu.VMEM((rows + 2 * H, 2 * levels, 128), f32)] * 6,
            pltpu.VMEM((gases, rows, 128), f32),
            pltpu.VMEM((gases, rows // 2, 128), f32),
            pltpu.VMEM((gases, rows // 2, 128), i16),
            pltpu.VMEM((chips - 1, gases, rows // 2, 128), i16),
            pltpu.VMEM((gases, rows // 2, 128), f32),
            pltpu.VMEM((gases, rows // 2, 128), f32),
            pltpu.VMEM((gases, rows // 2, 128), f32),
            pltpu.VMEM((8 * band_coef.shape[0], 128), bf16),
            pltpu.VMEM((rows, 128), f32),
            pltpu.SemaphoreType.DMA((2, levels)),
            pltpu.SemaphoreType.DMA((7,)),
            pltpu.SemaphoreType.DMA((n_copies,)),
            pltpu.SemaphoreType.DMA((n_copies,)),
        ],
        compiler_params=pltpu.CompilerParams(collective_id=0, has_side_effects=True, vmem_limit_bytes=40 * 2**20),
    )(
        *[pltpu.with_memory_space_constraint(a, pltpu.HBM) for a in operands]
    )


def solution(mesh):
    tiles = P(None, "grp", "gy", "gx")
    in_specs = (tiles, tiles, tiles, P("gy", "gx"), P(), P(), P(), P(), P())
    out_specs = (tiles, P("grp", "gy", "gx"))
    return jax.shard_map(shards, mesh=mesh, in_specs=in_specs, out_specs=out_specs, check_vma=False)
```

```python
import functools

import jax
import jax.numpy as jnp
from jax import lax
from jax.experimental import pallas as pl
from jax.experimental.pallas import tpu as pltpu
from jax.sharding import PartitionSpec as P

SUB = 8
RIM = 2
H = 2 * SUB
NDARK = 16
PLANES = 22
DIRECT = 10
MESH = pl.DeviceIdType.MESH
LOG2E = 1.4426950408889634


def encode(values, biggest):
    return jnp.round(values * (32700.0 * jnp.exp2(-biggest))).astype(jnp.int32).astype(jnp.int16)


def decode(codes, biggest):
    return codes.astype(jnp.int32).astype(jnp.float32) * (jnp.exp2(biggest) * (1.0 / 32700.0))


def exponent(values):
    top = jnp.max(jnp.abs(values), axis=0, keepdims=True)
    return jnp.ceil(jnp.log2(jnp.maximum(top, 1e-30)) + 1e-3)


def lane_ids(rows):
    return lax.broadcasted_iota(jnp.int32, (rows, 128), 1)


def turned(v, shift):
    lane = lax.broadcasted_iota(jnp.int32, v.shape, 2)
    same = pltpu.roll(v, shift % 128, 2)
    across = pltpu.roll(same, 4, 1)
    keep = lane >= shift if shift > 0 else lane < 128 + shift
    return jnp.where(keep, same, across)


def chunks(start, stop, size=8):
    return [(i, min(i + size, stop)) for i in range(start, stop, size)]


def substeps(wide, p, fx, fy, bx, by, st, out):
    rows = wide.shape[1] // 8

    def row(c, r):
        return wide[c, pl.ds(r, 8, stride=rows), :]

    for i, j in chunks(0, rows):
        for r in range(i, j):
            p[r] = row(2, r)
            st[r] = row(4, r)
            fy[r] = row(1, r)
            by[r] = row(3, r)
            if r > 0:
                fx[r - 1] = row(0, r)
                bx[r - 1] = by[r]
        fy[i:j] = turned(fy[i:j], -1)
        by[i:j] = turned(by[i:j], -1)
    first = 0
    pv, xv, yv = p[...], fx[0 : rows - 1], fy[...]
    for step in range(SUB):
        n = rows - 2 * first
        xv = xv[0 : n - 2] - bx[first : first + n - 2] * (pv[2:n] - pv[0 : n - 2])
        here = pv[2 : n - 2]
        inner = slice(first + 2, first + n - 2)
        yv = yv[2 : n - 2] - by[inner] * (turned(here, -2) - here)
        across = yv - turned(yv, 2)
        pv = here - st[inner] * ((xv[2 : n - 2] - xv[0 : n - 4]) + across)
        last, xv = xv, xv[2 : n - 2]
        first += 2
    own = rows - 2 * H
    moved = turned(yv, 1)
    for r in range(own):
        out[0, pl.ds(r, 8, stride=own), :] = last[r + 1]
        out[1, pl.ds(r, 8, stride=own), :] = moved[r]
        out[2, pl.ds(r, 8, stride=own), :] = pv[r]


def kernel(
    sizes,
    state, coefs, absorbers, route_row, band_rows, solar_row, mass_row, ridx_rows, rweight_rows,
    new_state, heating,
    route, band, solar, mass, ridx, rweight,
    wide, gas, rows_out, rows_in, sides_out, sides_in, corners_out, corners_in, exps, out, near, passing,
    p, fx, fy, bx, by, st, block_sum, sib, chip_sum, lower, part, rest, prefix, lhs, sunlit,
    tile_sem, in_sem, send_sem, recv_sem, ready,
):
    n_grp, n_gx, n_gy = sizes
    dyn_groups = 3 * n_grp // 4
    chips = n_grp // 2
    levels, rows = 4, 32
    me, gx, gy = lax.axis_index("grp"), lax.axis_index("gx"), lax.axis_index("gy")
    core, chip = lax.rem(me, 2), lax.div(me, 2)
    dyn = me < dyn_groups
    has_l, has_r = gx > 0, gx < n_gx - 1
    has_u, has_d = gy > 0, gy < n_gy - 1
    land = jnp.logical_and

    loads = [
        pltpu.make_async_copy(absorbers, gas, in_sem.at[0]),
        pltpu.make_async_copy(band_rows, band, in_sem.at[1]),
        pltpu.make_async_copy(solar_row, solar, in_sem.at[2]),
        pltpu.make_async_copy(route_row, route, in_sem.at[3]),
        pltpu.make_async_copy(ridx_rows, ridx, in_sem.at[4]),
        pltpu.make_async_copy(rweight_rows, rweight, in_sem.at[5]),
        pltpu.make_async_copy(mass_row, mass, in_sem.at[6]),
    ]
    tall_rows = rows + 2 * H
    tiles = []
    for l in range(levels):
        at = tall_rows * l + H
        tiles.append(pltpu.make_async_copy(state.at[:, l], wide.at[0:3, at : at + rows, :], tile_sem.at[0, l]))
        tiles.append(pltpu.make_async_copy(coefs.at[:, l], wide.at[3:5, at : at + rows, :], tile_sem.at[1, l]))
    for load in tiles:
        load.start()

    seam = n_gy // 2
    far = seam >= 2
    edge_d, edge_u = land(dyn, gy == seam - 1), land(dyn, gy == seam)
    first = me < 2
    pass_d = land(dyn, jnp.where(gy == seam - 1, me + 2 < dyn_groups, land(gy == seam - 2, first)))
    by_way = {"grp": jnp.where(first, me, me - 2), "gy": jnp.where(first, seam - 2, seam - 1)}
    beyond = {"grp": jnp.where(gy == seam - 1, me + 2, me), "gy": seam + 0 * gy}
    above_us, below_us = [], []
    for dx, cx in ((0, True), (-1, has_l), (1, has_r)):
        here = land(dyn, cx)
        above_us.append((land(here, has_u), {"gx": gx + dx, "gy": gy - 1}))
        below_us.append((land(here, has_d), {"gx": gx + dx, "gy": gy + 1}))
    aside = [
        (land(dyn, has_r), gx + 1 <= n_gx // 2, {"gx": gx + 1}),
        (land(dyn, has_l), gx - 1 >= n_gx // 2, {"gx": gx - 1}),
    ]
    same_tile = []
    for d in sorted({1} | {2 * d for d in range(1, chips)}):
        for other_me, cond in ((me + d, me + d < n_grp), (me - d, me - d >= 0)):
            other_chip = lax.div(jnp.maximum(other_me, 0), 2)
            farther = jnp.where(gy < seam, other_chip > chip, other_chip < chip)
            late = jnp.where(other_chip == chip, core == 1, farther)
            same_tile.append((cond, late, {"grp": other_me}))
    beside = aside + same_tile
    barrier = pltpu.get_barrier_semaphore()

    def signal(sem, cond, dev):
        @pl.when(cond)
        def _():
            pl.semaphore_signal(sem, inc=1, device_id=dev, device_id_type=MESH)

    def number_of(conds):
        return functools.reduce(lambda n, c: n + c.astype(jnp.int32), conds, jnp.int32(0))

    below_late, above_late = ~edge_d, edge_u
    for cond, dev in below_us:
        signal(barrier, land(cond, below_late), dev)
    for cond, dev in above_us:
        signal(barrier, land(cond, above_late), dev)
    for cond, late, dev in beside:
        signal(barrier, land(cond, late), dev)
    for load in loads:
        load.start()
    count = number_of([land(cond, ~late) for cond, late, _ in beside])
    count = count + number_of([land(cond, ~above_late) for cond, _ in above_us]) + number_of([land(cond, ~below_late) for cond, _ in below_us])
    if far:
        signal(barrier, edge_u, by_way)
        count = count + pass_d.astype(jnp.int32)

    number = [0]

    def remote(src, dst, dev, arrival=None):
        i = number[0]
        number[0] += 1
        return pltpu.make_async_remote_copy(
            src_ref=src,
            dst_ref=dst,
            send_sem=send_sem.at[i],
            recv_sem=recv_sem.at[i if arrival is None else arrival],
            device_id=dev,
            device_id_type=MESH,
        )

    def all_of(*conds):
        return functools.reduce(land, conds)

    down, up = all_of(dyn, has_d), all_of(dyn, has_u)
    rest_down = rows_out.at[DIRECT:PLANES, rows - H :]
    rest_up = rows_out.at[DIRECT:PLANES, 0:H]
    down_sem = number[0]
    by_down = (land(down, ~edge_d) if far else down, up, remote(rest_down, rows_in.at[0, DIRECT:PLANES], {"gy": gy + 1}))
    to_below = [(down, up, remote(rows_out.at[0:DIRECT, rows - H :], rows_in.at[0, 0:DIRECT], {"gy": gy + 1})), by_down]
    to_above = [
        (up, down, remote(rows_out.at[0:DIRECT, 0:H], rows_in.at[1, 0:DIRECT], {"gy": gy - 1})),
        (up, down, remote(rest_up, rows_in.at[1, DIRECT:PLANES], {"gy": gy - 1})),
    ]
    passes, relays = [], []
    if far:
        passes = [(edge_d, pass_d, remote(rest_down, passing, by_way))]
        relays = [(pass_d, None, remote(passing, rows_in.at[0, DIRECT:PLANES], beyond, down_sem))]
    to_sides = [
        (all_of(dyn, has_r), all_of(dyn, has_l), remote(sides_out.at[0], sides_in.at[0], {"gx": gx + 1})),
        (all_of(dyn, has_l), all_of(dyn, has_r), remote(sides_out.at[1], sides_in.at[1], {"gx": gx - 1})),
    ]
    for side, (to, back, dx) in enumerate(((has_r, has_l, 1), (has_l, has_r, -1))):
        bottom = corners_out.at[side, :, rows - H :]
        top = corners_out.at[side, :, 0:H]
        to_below.append(
            (all_of(dyn, to, has_d), all_of(dyn, back, has_u), remote(bottom, corners_in.at[side, 0], {"gx": gx + dx, "gy": gy + 1}))
        )
        to_above.append(
            (all_of(dyn, to, has_u), all_of(dyn, back, has_d), remote(top, corners_in.at[side, 1], {"gx": gx + dx, "gy": gy - 1}))
        )
    halo = to_below + to_above + to_sides
    half = rows // 2
    mine = pl.multiple_of(half * core, half)
    other = pl.multiple_of(half * (1 - core), half)
    sibling = {"grp": me + 1 - 2 * core}
    to_sib = remote(block_sum.at[:, pl.ds(other, half)], sib, sibling)
    to_chips = [
        (chip + d < chips, chip - d >= 0, remote(chip_sum, lower.at[d - 1], {"grp": me + 2 * d})) for d in range(1, chips)
    ]
    to_rest = remote(part, rest, sibling)
    remap = [
        (me > 0, me < n_grp - 1, remote(out.at[:, 0 : RIM * rows], near.at[1], {"grp": me - 1})),
        (me < n_grp - 1, me > 0, remote(out.at[:, (levels - RIM) * rows : levels * rows], near.at[0], {"grp": me + 1})),
    ]

    def start(item, when=None):
        @pl.when(item[0] if when is None else land(item[0], when))
        def _():
            item[2].start()

    def wait_recv(item):
        @pl.when(item[1])
        def _():
            item[2].wait_recv()

    def wait_send(item):
        @pl.when(item[0])
        def _():
            item[2].wait_send()

    @pl.when(count > 0)
    def _():
        pl.semaphore_wait(barrier, count)

    for cond, dev in above_us:
        signal(ready.at[0], land(cond, ~above_late), dev)
    for cond, dev in below_us:
        signal(ready.at[1], land(cond, ~below_late), dev)
    for cond, late, dev in aside:
        signal(ready.at[2], land(cond, ~late), dev)
    for cond, late, dev in same_tile:
        signal(ready.at[3], land(cond, ~late), dev)

    def await_ready(i, conds):
        n = number_of(conds)

        @pl.when(n > 0)
        def _():
            pl.semaphore_wait(ready.at[i], n)

    for load in tiles:
        load.wait()

    exps[...] = jnp.zeros(exps.shape, jnp.float32)
    for c in range(5):
        for l in range(levels):
            cells = wide[c, tall_rows * l + H : tall_rows * l + H + rows, :]
            biggest = exponent(cells)
            exps[levels * c + l : levels * c + l + 1, :] = biggest
            rows_out[levels * c + l] = encode(cells, biggest)
    for i in range(2):
        held = exps[16 * i : 16 * i + 16, :]
        rows_out[20 + i] = jnp.concatenate([held, held], axis=0).astype(jnp.int32).astype(jnp.int16)

    for item in passes:
        start(item)
    for item in to_below[:2]:
        start(item, ~below_late)
    for item in to_above[:2]:
        start(item, ~above_late)

    lane = lane_ids(rows)
    for q in range(3):
        right = jnp.zeros((rows, 128), jnp.float32)
        left = jnp.zeros((rows, 128), jnp.float32)
        for c in (2 * q, 2 * q + 1):
            if c > 4:
                continue
            for l in range(levels):
                t = 2 * l + c % 2
                cells = wide[c, tall_rows * l + H : tall_rows * l + H + rows, :]
                here = lax.div(lane, 16) == t
                shift = (16 * t + 16) % 128
                right = jnp.where(here, pltpu.roll(cells, shift, 1) if shift else cells, right)
                shift = 16 * t
                left = jnp.where(here, pltpu.roll(cells, shift, 1) if shift else cells, left)
        for side, strip in enumerate((right, left)):
            biggest = exponent(strip)
            sides_out[side, q, 0:rows] = encode(strip, biggest)
            sides_out[side, q, rows : rows + 16] = jnp.broadcast_to(biggest, (16, 128)).astype(jnp.int32).astype(jnp.int16)
            corners_out[side, q] = strip.astype(jnp.bfloat16)

    for item in to_below[2:]:
        start(item, ~below_late)
    for item in to_above[2:]:
        start(item, ~above_late)
    for item, relay in zip(passes, relays):
        wait_recv(item)
        start(relay)
    await_ready(2, [land(cond, late) for cond, late, _ in aside])
    for item in to_sides:
        start(item)

    loads[0].wait()
    for f in range(gas.shape[0]):
        total = gas[f, 0].astype(jnp.float32)
        for l in range(1, levels):
            total = total + gas[f, l].astype(jnp.float32)
        block_sum[f] = total
    await_ready(3, [land(cond, late) for cond, late, _ in same_tile])
    to_sib.start()

    await_ready(0, [land(cond, below_late) for cond, _ in below_us])
    for item in to_below:
        start(item, below_late)

    def fill(cond, ref, *index, value=0):
        @pl.when(cond)
        def _():
            view = ref.at[index] if index else ref
            view[...] = jnp.full(view.shape, value, view.dtype)

    fill(~has_u, rows_in, 0)
    fill(~has_d, rows_in, 1)
    fill(~has_l, sides_in, 0)
    fill(~has_r, sides_in, 1)
    fill(~land(has_l, has_u), corners_in, 0, 0)
    fill(~land(has_l, has_d), corners_in, 0, 1)
    fill(~land(has_r, has_u), corners_in, 1, 0)
    fill(~land(has_r, has_d), corners_in, 1, 1)
    fill(me == 0, near, 0)
    fill(me == n_grp - 1, near, 1)
    for d in range(1, chips):
        fill(chip - d < 0, lower, d - 1, value=-4 * 8191)

    @pl.when(~dyn)
    def _():
        for c in range(3):
            for l in range(levels):
                out[c, rows * l : rows * l + rows, :] = wide[c, tall_rows * l + H : tall_rows * l + H + rows, :]

    for load in loads[1:]:
        load.wait()
    gases, gpoints = band.shape
    r0 = lax.broadcasted_iota(jnp.int32, (gpoints, gpoints), 0)
    r1 = lax.broadcasted_iota(jnp.int32, (gpoints, gpoints), 1)
    logs = jnp.log2(solar[...])
    high = logs.astype(jnp.bfloat16).astype(jnp.float32)
    middle = (logs - high).astype(jnp.bfloat16).astype(jnp.float32)
    low = logs - high - middle
    srcs = jnp.concatenate([band[...].astype(jnp.float32), high, middle, low], axis=0).astype(jnp.bfloat16)
    n_src = gases + 3
    l0 = lax.broadcasted_iota(jnp.int32, (rows, rows), 0)
    l1 = lax.broadcasted_iota(jnp.int32, (rows, rows), 1)
    lit_row = jnp.broadcast_to((route[...] < NDARK).astype(jnp.float32), (rows, rows))
    sunlit[...] = jnp.broadcast_to(jnp.sum(jnp.where(l0 == l1, lit_row, 0.0), axis=1, keepdims=True), (rows, 128))
    spread0 = lax.div(lax.broadcasted_iota(jnp.int32, (8 * gpoints, gpoints), 0), 8)
    spread1 = lax.broadcasted_iota(jnp.int32, (8 * gpoints, gpoints), 1)
    spread = (spread0 == spread1).astype(jnp.float32).astype(jnp.bfloat16)
    tall = lax.dot_general(spread, srcs, (((1,), (1,)), ((), ())), preferred_element_type=jnp.float32).astype(jnp.bfloat16)
    w0 = lax.broadcasted_iota(jnp.int32, (n_src, 128), 0)
    w1 = lax.broadcasted_iota(jnp.int32, (n_src, 128), 1)
    in_gas = w1 < 16 * gases
    owner = jnp.where(in_gas, lax.rem(lax.div(w1, 8), gases), w1 - 16 * gases + gases)
    widen = (w0 == owner).astype(jnp.float32).astype(jnp.bfloat16)
    spread_all = jnp.dot(tall, widen, preferred_element_type=jnp.float32)
    m0 = lax.broadcasted_iota(jnp.int32, (8 * gpoints, 128), 0)
    m1 = lax.broadcasted_iota(jnp.int32, (8 * gpoints, 128), 1)
    keep = (m1 >= 16 * gases) | (lax.rem(m0, 8) == lax.rem(m1, 8))
    lhs[...] = jnp.where(keep, spread_all, 0.0).astype(jnp.bfloat16)

    to_sib.wait_recv()
    both = block_sum[:, pl.ds(mine, half), :] + sib[...]
    chip_sum[...] = jnp.round((both - 4.0) * 8191.0).astype(jnp.int32).astype(jnp.int16)
    for item in to_chips:
        start(item)

    def radiate(start_row, ref):
        columns = []
        for g in range(half // 8):
            depth = ref[:, 8 * g : 8 * g + 8, :]
            for l in range(levels + 1):
                if l:
                    cells = gas[:, l - 1, pl.ds(start_row, half), :].astype(jnp.float32)
                    depth = depth + cells[:, 8 * g : 8 * g + 8, :]
                scaled = (depth * -LOG2E).reshape(8 * gases, 128)
                high = scaled.astype(jnp.bfloat16).astype(jnp.float32)
                stack = jnp.concatenate([high, scaled - high, jnp.ones((128 - 16 * gases, 128), jnp.float32)], axis=0)
                columns.append(stack.astype(jnp.bfloat16))
        cols = jnp.concatenate(columns, axis=1)
        expo = jnp.dot(lhs[...], cols, preferred_element_type=jnp.float32)
        flux = jnp.sum(jnp.exp2(expo).reshape(gpoints, 8, cols.shape[1]), axis=0)
        for l in range(levels):
            parts = []
            for g in range(half // 8):
                at = 128 * (g * (levels + 1) + l)
                parts.append(flux[:, at : at + 128] - flux[:, at + 128 : at + 256])
            diff = jnp.concatenate(parts, axis=0)
            lit = sunlit[pl.ds(start_row, half), :] > 0.5
            rate = diff / jnp.full((half, 128), mass[0, levels * me + l])
            heating[l, pl.ds(start_row, half), :] = jnp.where(lit, rate, 0.0)

    def shine():
        for item in to_chips:
            wait_recv(item)
        above = jnp.zeros(rest.shape, jnp.float32)
        for d in range(1, chips):
            above = above + (lower[d - 1].astype(jnp.int32).astype(jnp.float32) * (1.0 / 8191.0) + 4.0)
        even = (core == 0).astype(jnp.float32)
        part[...] = above + even * block_sum[:, pl.ds(mine, half), :]
        to_rest.start()
        prefix[...] = above + (1.0 - even) * sib[...]
        radiate(mine, prefix)
        to_rest.wait_recv()
        radiate(other, rest)

    waits = land(gy >= seam - 1, gy <= seam)

    @pl.when(waits)
    def _():
        shine()

    await_ready(1, [land(cond, above_late) for cond, _ in above_us])
    for item in to_above:
        start(item, above_late)
    for item in halo:
        wait_recv(item)

    @pl.when(dyn)
    def _():
        for i, at in enumerate((0, H + rows)):
            biggest = jnp.concatenate([rows_in[i, 20], rows_in[i, 21]], axis=0).astype(jnp.int32).astype(jnp.float32)
            exps[...] = biggest
            for c in range(5):
                for l in range(levels):
                    k = levels * c + l
                    wide[c, tall_rows * l + at : tall_rows * l + at + H, :] = decode(rows_in[i, k], exps[k : k + 1, :])
        lane_w = lane_ids(rows + 2 * H)
        for q in range(3):
            strips = []
            for side in range(2):
                biggest = sides_in[side, q, rows : rows + 16].astype(jnp.int32).astype(jnp.float32)[0:1]
                middle = decode(sides_in[side, q, 0:rows], biggest)
                ends = [corners_in[side, i, q].astype(jnp.float32) for i in range(2)]
                strips.append(jnp.concatenate([ends[0], middle, ends[1]], axis=0))
            for c in (2 * q, 2 * q + 1):
                if c > 4:
                    continue
                for l in range(levels):
                    t = 2 * l + c % 2
                    shift = (112 - 16 * t) % 128
                    left = pltpu.roll(strips[0], shift, 1) if shift else strips[0]
                    shift = (128 - 16 * t) % 128
                    right = pltpu.roll(strips[1], shift, 1) if shift else strips[1]
                    wide[c, tall_rows * (levels + l) : tall_rows * (levels + l + 1), :] = jnp.where(
                        lane_w < 16, right, jnp.where(lane_w >= 112, left, 0.0)
                    )
        substeps(wide, p, fx, fy, bx, by, st, out)

    for item in remap:
        start(item)

    @pl.when(~waits)
    def _():
        shine()

    for item in remap:
        wait_recv(item)
    for kl in range(levels):
        k = levels * me + kl
        weights = []
        for o in range(-RIM, RIM + 1):
            w = jnp.float32(0)
            for j in range(ridx.shape[0]):
                w = w + jnp.where(ridx[j, k] == k + o, rweight[j, k], jnp.float32(0))
            weights.append(w)
        for c in range(3):
            acc = jnp.zeros((rows, 128), jnp.float32)
            for o in range(-RIM, RIM + 1):
                m = kl + o
                ref, m = (near.at[0], m + RIM) if m < 0 else (out, m) if m < levels else (near.at[1], m - levels)
                cells = ref[c, rows * m : rows * m + rows, :]
                acc = acc + weights[o + RIM] * cells
            new_state[c, kl] = acc

    for item in passes + relays + halo + to_chips + remap:
        wait_send(item)
    to_sib.wait_send()
    to_rest.wait_send()


def shards(state, coefs, lagged_absorbers, sun_route, band_coef, solar, layer_mass, remap_index, remap_weight):
    sizes = tuple(lax.axis_size(a) for a in ("grp", "gx", "gy"))
    chips = sizes[0] // 2
    gases = lagged_absorbers.shape[0]
    levels, rows = state.shape[1:3]
    f32, bf16, i16 = jnp.float32, jnp.bfloat16, jnp.int16
    operands = (
        state, coefs, lagged_absorbers, sun_route.T, band_coef.T, solar.reshape(1, -1), layer_mass.reshape(1, -1),
        remap_index.T, remap_weight.T,
    )
    n_copies = 14 + 1 + (chips - 1) + 1 + 2
    return pl.pallas_call(
        functools.partial(kernel, sizes),
        out_shape=(jax.ShapeDtypeStruct(state.shape, f32), jax.ShapeDtypeStruct(state.shape[1:], f32)),
        in_specs=[pl.BlockSpec(memory_space=pltpu.HBM)] * len(operands),
        out_specs=(pl.BlockSpec(memory_space=pltpu.VMEM),) * 2,
        scratch_shapes=[
            pltpu.VMEM((1, rows), jnp.int32),
            pltpu.VMEM(band_coef.shape[::-1], bf16),
            pltpu.VMEM((1, solar.shape[0]), f32),
            pltpu.SMEM((1, layer_mass.shape[0]), f32),
            pltpu.SMEM(remap_index.shape[::-1], jnp.int32),
            pltpu.SMEM(remap_weight.shape[::-1], f32),
            pltpu.VMEM((5, 2 * levels * (rows + 2 * H), 128), f32),
            pltpu.VMEM(lagged_absorbers.shape, bf16),
            pltpu.VMEM((PLANES, rows, 128), i16),
            pltpu.VMEM((2, PLANES, H, 128), i16),
            pltpu.VMEM((2, 3, rows + 16, 128), i16),
            pltpu.VMEM((2, 3, rows + 16, 128), i16),
            pltpu.VMEM((2, 3, rows, 128), bf16),
            pltpu.VMEM((2, 2, 3, H, 128), bf16),
            pltpu.VMEM((32, 128), f32),
            pltpu.VMEM((3, 2 * levels * rows, 128), f32),
            pltpu.VMEM((2, 3, RIM * rows, 128), f32),
            pltpu.VMEM((PLANES - DIRECT, H, 128), i16),
            *[pltpu.VMEM((rows + 2 * H, 2 * levels, 128), f32)] * 6,
            pltpu.VMEM((gases, rows, 128), f32),
            pltpu.VMEM((gases, rows // 2, 128), f32),
            pltpu.VMEM((gases, rows // 2, 128), i16),
            pltpu.VMEM((chips - 1, gases, rows // 2, 128), i16),
            pltpu.VMEM((gases, rows // 2, 128), f32),
            pltpu.VMEM((gases, rows // 2, 128), f32),
            pltpu.VMEM((gases, rows // 2, 128), f32),
            pltpu.VMEM((8 * band_coef.shape[0], 128), bf16),
            pltpu.VMEM((rows, 128), f32),
            pltpu.SemaphoreType.DMA((2, levels)),
            pltpu.SemaphoreType.DMA((7,)),
            pltpu.SemaphoreType.DMA((n_copies,)),
            pltpu.SemaphoreType.DMA((n_copies,)),
            pltpu.SemaphoreType.REGULAR((4,)),
        ],
        compiler_params=pltpu.CompilerParams(collective_id=0, has_side_effects=True, vmem_limit_bytes=40 * 2**20),
    )(
        *[pltpu.with_memory_space_constraint(a, pltpu.HBM) for a in operands]
    )


def solution(mesh):
    tiles = P(None, "grp", "gy", "gx")
    in_specs = (tiles, tiles, tiles, P("gy", "gx"), P(), P(), P(), P(), P())
    out_specs = (tiles, P("grp", "gy", "gx"))
    return jax.shard_map(shards, mesh=mesh, in_specs=in_specs, out_specs=out_specs, check_vma=False)
```

```python
import functools

import jax
import jax.numpy as jnp
from jax import lax
from jax.experimental import pallas as pl
from jax.experimental.pallas import tpu as pltpu
from jax.sharding import PartitionSpec as P

SUB = 8
RIM = 2
H = 2 * SUB
NDARK = 16
PLANES = 22
DIRECT = 10
MESH = pl.DeviceIdType.MESH
LOG2E = 1.4426950408889634


def encode(values, biggest):
    return jnp.round(values * (32700.0 * jnp.exp2(-biggest))).astype(jnp.int32).astype(jnp.int16)


def decode(codes, biggest):
    return codes.astype(jnp.int32).astype(jnp.float32) * (jnp.exp2(biggest) * (1.0 / 32700.0))


def exponent(values):
    top = jnp.max(jnp.abs(values), axis=0, keepdims=True)
    return jnp.ceil(jnp.log2(jnp.maximum(top, 1e-30)) + 1e-3)


def lane_ids(rows):
    return lax.broadcasted_iota(jnp.int32, (rows, 128), 1)


def turned(v, shift):
    lane = lax.broadcasted_iota(jnp.int32, v.shape, 2)
    same = pltpu.roll(v, shift % 128, 2)
    across = pltpu.roll(same, 4, 1)
    keep = lane >= shift if shift > 0 else lane < 128 + shift
    return jnp.where(keep, same, across)


def chunks(start, stop, size=8):
    return [(i, min(i + size, stop)) for i in range(start, stop, size)]


def substeps(wide, base, p, fx, fy, bx, by, st, out):
    rows = p.shape[0]
    tall_rows = wide.shape[1] // 8

    def row(c, r):
        return wide[c, pl.ds(base + r, 8, stride=tall_rows), :]

    for i, j in chunks(0, rows):
        for r in range(i, j):
            p[r] = row(2, r)
            st[r] = row(4, r)
            fy[r] = row(1, r)
            by[r] = row(3, r)
            if r > 0:
                fx[r - 1] = row(0, r)
                bx[r - 1] = by[r]
        fy[i:j] = turned(fy[i:j], -1)
        by[i:j] = turned(by[i:j], -1)
    first = 0
    pv, xv, yv = p[...], fx[0 : rows - 1], fy[...]
    for step in range(SUB):
        n = rows - 2 * first
        xv = xv[0 : n - 2] - bx[first : first + n - 2] * (pv[2:n] - pv[0 : n - 2])
        here = pv[2 : n - 2]
        inner = slice(first + 2, first + n - 2)
        yv = yv[2 : n - 2] - by[inner] * (turned(here, -2) - here)
        across = yv - turned(yv, 2)
        pv = here - st[inner] * ((xv[2 : n - 2] - xv[0 : n - 4]) + across)
        last, xv = xv, xv[2 : n - 2]
        first += 2
    own = rows - 2 * H
    moved = turned(yv, 1)
    for r in range(own):
        out[0, pl.ds(r, 8, stride=own), :] = last[r + 1]
        out[1, pl.ds(r, 8, stride=own), :] = moved[r]
        out[2, pl.ds(r, 8, stride=own), :] = pv[r]


def kernel(
    sizes,
    state, coefs, absorbers, route_row, band_rows, solar_row, mass_row, ridx_rows, rweight_rows,
    new_state, heating,
    route, band, solar, mass, ridx, rweight,
    wide, gas, rows_out, rows_in, sides_out, sides_in, corners_out, corners_in, exps, out, near, passing,
    p, fx, fy, bx, by, st, block_sum, sib, chip_sum, lower, part, rest, prefix, lhs, sunlit,
    tile_sem, in_sem, send_sem, recv_sem, ready,
):
    n_grp, n_gx, n_gy = sizes
    dyn_groups = 3 * n_grp // 4
    chips = n_grp // 2
    levels, rows = 4, 32
    me, gx, gy = lax.axis_index("grp"), lax.axis_index("gx"), lax.axis_index("gy")
    core, chip = lax.rem(me, 2), lax.div(me, 2)
    dyn = me < dyn_groups
    has_l, has_r = gx > 0, gx < n_gx - 1
    has_u, has_d = gy > 0, gy < n_gy - 1
    land = jnp.logical_and

    loads = [
        pltpu.make_async_copy(absorbers, gas, in_sem.at[0]),
        pltpu.make_async_copy(band_rows, band, in_sem.at[1]),
        pltpu.make_async_copy(solar_row, solar, in_sem.at[2]),
        pltpu.make_async_copy(route_row, route, in_sem.at[3]),
        pltpu.make_async_copy(ridx_rows, ridx, in_sem.at[4]),
        pltpu.make_async_copy(rweight_rows, rweight, in_sem.at[5]),
        pltpu.make_async_copy(mass_row, mass, in_sem.at[6]),
    ]
    tall_rows = rows + 2 * H
    tiles = []
    for l in range(levels):
        at = tall_rows * l + H
        tiles.append(pltpu.make_async_copy(state.at[:, l], wide.at[0:3, at : at + rows, :], tile_sem.at[0, l]))
        tiles.append(pltpu.make_async_copy(coefs.at[:, l], wide.at[3:5, at : at + rows, :], tile_sem.at[1, l]))
    for load in tiles:
        load.start()

    seam = n_gy // 2
    far = seam >= 2
    edge_d, edge_u = land(dyn, gy == seam - 1), land(dyn, gy == seam)
    first = me < 2
    pass_d = land(dyn, jnp.where(gy == seam - 1, me + 2 < dyn_groups, land(gy == seam - 2, first)))
    by_way = {"grp": jnp.where(first, me, me - 2), "gy": jnp.where(first, seam - 2, seam - 1)}
    beyond = {"grp": jnp.where(gy == seam - 1, me + 2, me), "gy": seam + 0 * gy}
    above_us, below_us = [], []
    for dx, cx in ((0, True), (-1, has_l), (1, has_r)):
        here = land(dyn, cx)
        above_us.append((land(here, has_u), {"gx": gx + dx, "gy": gy - 1}))
        below_us.append((land(here, has_d), {"gx": gx + dx, "gy": gy + 1}))
    aside = [
        (land(dyn, has_r), gx + 1 <= n_gx // 2, {"gx": gx + 1}),
        (land(dyn, has_l), gx - 1 >= n_gx // 2, {"gx": gx - 1}),
    ]
    same_tile = []
    for d in sorted({1} | {2 * d for d in range(1, chips)}):
        for other_me, cond in ((me + d, me + d < n_grp), (me - d, me - d >= 0)):
            other_chip = lax.div(jnp.maximum(other_me, 0), 2)
            farther = jnp.where(gy < seam, other_chip > chip, other_chip < chip)
            late = jnp.where(other_chip == chip, core == 1, farther)
            same_tile.append((cond, late, {"grp": other_me}))
    beside = aside + same_tile
    barrier = pltpu.get_barrier_semaphore()

    def signal(sem, cond, dev):
        @pl.when(cond)
        def _():
            pl.semaphore_signal(sem, inc=1, device_id=dev, device_id_type=MESH)

    def number_of(conds):
        return functools.reduce(lambda n, c: n + c.astype(jnp.int32), conds, jnp.int32(0))

    below_late, above_late = ~edge_d, edge_u
    for cond, dev in below_us:
        signal(barrier, land(cond, below_late), dev)
    for cond, dev in above_us:
        signal(barrier, land(cond, above_late), dev)
    for cond, late, dev in beside:
        signal(barrier, land(cond, late), dev)
    for load in loads:
        load.start()
    count = number_of([land(cond, ~late) for cond, late, _ in beside])
    count = count + number_of([land(cond, ~above_late) for cond, _ in above_us]) + number_of([land(cond, ~below_late) for cond, _ in below_us])
    if far:
        signal(barrier, edge_u, by_way)
        count = count + pass_d.astype(jnp.int32)

    number = [0]

    def remote(src, dst, dev, arrival=None):
        i = number[0]
        number[0] += 1
        return pltpu.make_async_remote_copy(
            src_ref=src,
            dst_ref=dst,
            send_sem=send_sem.at[i],
            recv_sem=recv_sem.at[i if arrival is None else arrival],
            device_id=dev,
            device_id_type=MESH,
        )

    def all_of(*conds):
        return functools.reduce(land, conds)

    down, up = all_of(dyn, has_d), all_of(dyn, has_u)
    rest_down = rows_out.at[DIRECT:PLANES, rows - H :]
    rest_up = rows_out.at[DIRECT:PLANES, 0:H]
    down_sem = number[0]
    by_down = (land(down, ~edge_d) if far else down, up, remote(rest_down, rows_in.at[0, DIRECT:PLANES], {"gy": gy + 1}))
    to_below = [(down, up, remote(rows_out.at[0:DIRECT, rows - H :], rows_in.at[0, 0:DIRECT], {"gy": gy + 1})), by_down]
    to_above = [
        (up, down, remote(rows_out.at[0:DIRECT, 0:H], rows_in.at[1, 0:DIRECT], {"gy": gy - 1})),
        (up, down, remote(rest_up, rows_in.at[1, DIRECT:PLANES], {"gy": gy - 1})),
    ]
    passes, relays = [], []
    if far:
        passes = [(edge_d, pass_d, remote(rest_down, passing, by_way))]
        relays = [(pass_d, None, remote(passing, rows_in.at[0, DIRECT:PLANES], beyond, down_sem))]
    to_sides = [
        (all_of(dyn, has_r), all_of(dyn, has_l), remote(sides_out.at[0], sides_in.at[0], {"gx": gx + 1})),
        (all_of(dyn, has_l), all_of(dyn, has_r), remote(sides_out.at[1], sides_in.at[1], {"gx": gx - 1})),
    ]
    for side, (to, back, dx) in enumerate(((has_r, has_l, 1), (has_l, has_r, -1))):
        bottom = corners_out.at[side, :, rows - H :]
        top = corners_out.at[side, :, 0:H]
        to_below.append(
            (all_of(dyn, to, has_d), all_of(dyn, back, has_u), remote(bottom, corners_in.at[side, 0], {"gx": gx + dx, "gy": gy + 1}))
        )
        to_above.append(
            (all_of(dyn, to, has_u), all_of(dyn, back, has_d), remote(top, corners_in.at[side, 1], {"gx": gx + dx, "gy": gy - 1}))
        )
    halo = to_below + to_above + to_sides
    half = rows // 2
    mine = pl.multiple_of(half * core, half)
    other = pl.multiple_of(half * (1 - core), half)
    sibling = {"grp": me + 1 - 2 * core}
    to_sib = remote(block_sum.at[:, pl.ds(other, half)], sib, sibling)
    to_chips = [
        (chip + d < chips, chip - d >= 0, remote(chip_sum, lower.at[d - 1], {"grp": me + 2 * d})) for d in range(1, chips)
    ]
    to_rest = remote(part, rest, sibling)
    remap = [
        [
            (me > 0, me < n_grp - 1, remote(out.at[h, :, 0 : RIM * half], near.at[1, h], {"grp": me - 1})),
            (me < n_grp - 1, me > 0, remote(out.at[h, :, (levels - RIM) * half : levels * half], near.at[0, h], {"grp": me + 1})),
        ]
        for h in range(2)
    ]

    def start(item, when=None):
        @pl.when(item[0] if when is None else land(item[0], when))
        def _():
            item[2].start()

    def wait_recv(item):
        @pl.when(item[1])
        def _():
            item[2].wait_recv()

    def wait_send(item):
        @pl.when(item[0])
        def _():
            item[2].wait_send()

    @pl.when(count > 0)
    def _():
        pl.semaphore_wait(barrier, count)

    for cond, dev in above_us:
        signal(ready.at[0], land(cond, ~above_late), dev)
    for cond, dev in below_us:
        signal(ready.at[1], land(cond, ~below_late), dev)
    for cond, late, dev in aside:
        signal(ready.at[2], land(cond, ~late), dev)
    for cond, late, dev in same_tile:
        signal(ready.at[3], land(cond, ~late), dev)

    def await_ready(i, conds):
        n = number_of(conds)

        @pl.when(n > 0)
        def _():
            pl.semaphore_wait(ready.at[i], n)

    for load in tiles:
        load.wait()

    exps[...] = jnp.zeros(exps.shape, jnp.float32)
    for c in range(5):
        for l in range(levels):
            cells = wide[c, tall_rows * l + H : tall_rows * l + H + rows, :]
            biggest = exponent(cells)
            exps[levels * c + l : levels * c + l + 1, :] = biggest
            rows_out[levels * c + l] = encode(cells, biggest)
    for i in range(2):
        held = exps[16 * i : 16 * i + 16, :]
        rows_out[20 + i] = jnp.concatenate([held, held], axis=0).astype(jnp.int32).astype(jnp.int16)

    for item in passes:
        start(item)
    for item in to_below[:2]:
        start(item, ~below_late)
    for item in to_above[:2]:
        start(item, ~above_late)

    lane = lane_ids(rows)
    for q in range(3):
        right = jnp.zeros((rows, 128), jnp.float32)
        left = jnp.zeros((rows, 128), jnp.float32)
        for c in (2 * q, 2 * q + 1):
            if c > 4:
                continue
            for l in range(levels):
                t = 2 * l + c % 2
                cells = wide[c, tall_rows * l + H : tall_rows * l + H + rows, :]
                here = lax.div(lane, 16) == t
                shift = (16 * t + 16) % 128
                right = jnp.where(here, pltpu.roll(cells, shift, 1) if shift else cells, right)
                shift = 16 * t
                left = jnp.where(here, pltpu.roll(cells, shift, 1) if shift else cells, left)
        for side, strip in enumerate((right, left)):
            biggest = exponent(strip)
            sides_out[side, q, 0:rows] = encode(strip, biggest)
            sides_out[side, q, rows : rows + 16] = jnp.broadcast_to(biggest, (16, 128)).astype(jnp.int32).astype(jnp.int16)
            corners_out[side, q] = strip.astype(jnp.bfloat16)

    for item in to_below[2:]:
        start(item, ~below_late)
    for item in to_above[2:]:
        start(item, ~above_late)
    for item, relay in zip(passes, relays):
        wait_recv(item)
        start(relay)
    await_ready(2, [land(cond, late) for cond, late, _ in aside])
    for item in to_sides:
        start(item)

    loads[0].wait()
    for f in range(gas.shape[0]):
        total = gas[f, 0].astype(jnp.float32)
        for l in range(1, levels):
            total = total + gas[f, l].astype(jnp.float32)
        block_sum[f] = total
    await_ready(3, [land(cond, late) for cond, late, _ in same_tile])
    to_sib.start()

    await_ready(0, [land(cond, below_late) for cond, _ in below_us])
    for item in to_below:
        start(item, below_late)

    def fill(cond, ref, *index, value=0):
        @pl.when(cond)
        def _():
            view = ref.at[index] if index else ref
            view[...] = jnp.full(view.shape, value, view.dtype)

    fill(~has_u, rows_in, 0)
    fill(~has_d, rows_in, 1)
    fill(~has_l, sides_in, 0)
    fill(~has_r, sides_in, 1)
    fill(~land(has_l, has_u), corners_in, 0, 0)
    fill(~land(has_l, has_d), corners_in, 0, 1)
    fill(~land(has_r, has_u), corners_in, 1, 0)
    fill(~land(has_r, has_d), corners_in, 1, 1)
    fill(me == 0, near, 0)
    fill(me == n_grp - 1, near, 1)
    for d in range(1, chips):
        fill(chip - d < 0, lower, d - 1, value=-4 * 8191)

    @pl.when(~dyn)
    def _():
        for c in range(3):
            for l in range(levels):
                for h in range(2):
                    at = tall_rows * l + H + half * h
                    out[h, c, half * l : half * l + half, :] = wide[c, at : at + half, :]

    for load in loads[1:]:
        load.wait()
    gases, gpoints = band.shape
    r0 = lax.broadcasted_iota(jnp.int32, (gpoints, gpoints), 0)
    r1 = lax.broadcasted_iota(jnp.int32, (gpoints, gpoints), 1)
    logs = jnp.log2(solar[...])
    high = logs.astype(jnp.bfloat16).astype(jnp.float32)
    middle = (logs - high).astype(jnp.bfloat16).astype(jnp.float32)
    low = logs - high - middle
    srcs = jnp.concatenate([band[...].astype(jnp.float32), high, middle, low], axis=0).astype(jnp.bfloat16)
    n_src = gases + 3
    l0 = lax.broadcasted_iota(jnp.int32, (rows, rows), 0)
    l1 = lax.broadcasted_iota(jnp.int32, (rows, rows), 1)
    lit_row = jnp.broadcast_to((route[...] < NDARK).astype(jnp.float32), (rows, rows))
    sunlit[...] = jnp.broadcast_to(jnp.sum(jnp.where(l0 == l1, lit_row, 0.0), axis=1, keepdims=True), (rows, 128))
    spread0 = lax.div(lax.broadcasted_iota(jnp.int32, (8 * gpoints, gpoints), 0), 8)
    spread1 = lax.broadcasted_iota(jnp.int32, (8 * gpoints, gpoints), 1)
    spread = (spread0 == spread1).astype(jnp.float32).astype(jnp.bfloat16)
    tall = lax.dot_general(spread, srcs, (((1,), (1,)), ((), ())), preferred_element_type=jnp.float32).astype(jnp.bfloat16)
    w0 = lax.broadcasted_iota(jnp.int32, (n_src, 128), 0)
    w1 = lax.broadcasted_iota(jnp.int32, (n_src, 128), 1)
    in_gas = w1 < 16 * gases
    owner = jnp.where(in_gas, lax.rem(lax.div(w1, 8), gases), w1 - 16 * gases + gases)
    widen = (w0 == owner).astype(jnp.float32).astype(jnp.bfloat16)
    spread_all = jnp.dot(tall, widen, preferred_element_type=jnp.float32)
    m0 = lax.broadcasted_iota(jnp.int32, (8 * gpoints, 128), 0)
    m1 = lax.broadcasted_iota(jnp.int32, (8 * gpoints, 128), 1)
    keep = (m1 >= 16 * gases) | (lax.rem(m0, 8) == lax.rem(m1, 8))
    lhs[...] = jnp.where(keep, spread_all, 0.0).astype(jnp.bfloat16)

    to_sib.wait_recv()
    both = block_sum[:, pl.ds(mine, half), :] + sib[...]
    chip_sum[...] = jnp.round((both - 4.0) * 8191.0).astype(jnp.int32).astype(jnp.int16)
    for item in to_chips:
        start(item)

    def radiate(start_row, ref):
        columns = []
        for g in range(half // 8):
            depth = ref[:, 8 * g : 8 * g + 8, :]
            for l in range(levels + 1):
                if l:
                    cells = gas[:, l - 1, pl.ds(start_row, half), :].astype(jnp.float32)
                    depth = depth + cells[:, 8 * g : 8 * g + 8, :]
                scaled = (depth * -LOG2E).reshape(8 * gases, 128)
                high = scaled.astype(jnp.bfloat16).astype(jnp.float32)
                stack = jnp.concatenate([high, scaled - high, jnp.ones((128 - 16 * gases, 128), jnp.float32)], axis=0)
                columns.append(stack.astype(jnp.bfloat16))
        cols = jnp.concatenate(columns, axis=1)
        expo = jnp.dot(lhs[...], cols, preferred_element_type=jnp.float32)
        flux = jnp.sum(jnp.exp2(expo).reshape(gpoints, 8, cols.shape[1]), axis=0)
        for l in range(levels):
            parts = []
            for g in range(half // 8):
                at = 128 * (g * (levels + 1) + l)
                parts.append(flux[:, at : at + 128] - flux[:, at + 128 : at + 256])
            diff = jnp.concatenate(parts, axis=0)
            lit = sunlit[pl.ds(start_row, half), :] > 0.5
            rate = diff / jnp.full((half, 128), mass[0, levels * me + l])
            heating[l, pl.ds(start_row, half), :] = jnp.where(lit, rate, 0.0)

    def shine():
        for item in to_chips:
            wait_recv(item)
        above = jnp.zeros(rest.shape, jnp.float32)
        for d in range(1, chips):
            above = above + (lower[d - 1].astype(jnp.int32).astype(jnp.float32) * (1.0 / 8191.0) + 4.0)
        even = (core == 0).astype(jnp.float32)
        part[...] = above + even * block_sum[:, pl.ds(mine, half), :]
        to_rest.start()
        prefix[...] = above + (1.0 - even) * sib[...]
        radiate(mine, prefix)
        to_rest.wait_recv()
        radiate(other, rest)

    waits = land(gy >= seam - 1, gy <= seam)

    @pl.when(waits)
    def _():
        shine()

    lane_h = lane_ids(rows + H)

    def decode_rows(i, at):
        exps[...] = jnp.concatenate([rows_in[i, 20], rows_in[i, 21]], axis=0).astype(jnp.int32).astype(jnp.float32)
        for c in range(5):
            for l in range(levels):
                k = levels * c + l
                wide[c, tall_rows * l + at : tall_rows * l + at + H, :] = decode(rows_in[i, k], exps[k : k + 1, :])

    def place_sides(q, strips, at):
        n = strips[0].shape[0]
        for c in (2 * q, 2 * q + 1):
            if c > 4:
                continue
            for l in range(levels):
                t = 2 * l + c % 2
                shift = (112 - 16 * t) % 128
                left = pltpu.roll(strips[0], shift, 1) if shift else strips[0]
                shift = (128 - 16 * t) % 128
                right = pltpu.roll(strips[1], shift, 1) if shift else strips[1]
                start_row = tall_rows * (levels + l) + at
                wide[c, start_row : start_row + n, :] = jnp.where(
                    lane_h[0:n] < 16, right, jnp.where(lane_h[0:n] >= 112, left, 0.0)
                )

    for item in to_above + to_sides:
        wait_recv(item)

    @pl.when(dyn)
    def _():
        decode_rows(1, H + rows)
        for q in range(3):
            strips = []
            for side in range(2):
                biggest = sides_in[side, q, rows : rows + 16].astype(jnp.int32).astype(jnp.float32)[0:1]
                middle = decode(sides_in[side, q, 0:rows], biggest)
                strips.append(jnp.concatenate([middle, corners_in[side, 1, q].astype(jnp.float32)], axis=0))
            place_sides(q, strips, H)
        substeps(wide, half, p, fx, fy, bx, by, st, out.at[1])

    for item in remap[1]:
        start(item)
    await_ready(1, [land(cond, above_late) for cond, _ in above_us])
    for item in to_above:
        start(item, above_late)

    for item in to_below:
        wait_recv(item)

    @pl.when(dyn)
    def _():
        decode_rows(0, 0)
        for q in range(3):
            place_sides(q, [corners_in[side, 0, q].astype(jnp.float32) for side in range(2)], 0)
        substeps(wide, 0, p, fx, fy, bx, by, st, out.at[0])

    for item in remap[0]:
        start(item)

    @pl.when(~waits)
    def _():
        shine()

    weights = []
    for kl in range(levels):
        k = levels * me + kl
        for o in range(-RIM, RIM + 1):
            w = jnp.float32(0)
            for j in range(ridx.shape[0]):
                w = w + jnp.where(ridx[j, k] == k + o, rweight[j, k], jnp.float32(0))
            weights.append(w)
    for h in (1, 0):
        for item in remap[h]:
            wait_recv(item)
        for kl in range(levels):
            for c in range(3):
                acc = jnp.zeros((half, 128), jnp.float32)
                for o in range(-RIM, RIM + 1):
                    m = kl + o
                    if m < 0:
                        cells = near[0, h, c, half * (m + RIM) : half * (m + RIM + 1), :]
                    elif m < levels:
                        cells = out[h, c, half * m : half * m + half, :]
                    else:
                        cells = near[1, h, c, half * (m - levels) : half * (m - levels + 1), :]
                    acc = acc + weights[(2 * RIM + 1) * kl + o + RIM] * cells
                new_state[c, kl, half * h : half * h + half, :] = acc

    for item in passes + relays + halo + to_chips + remap[0] + remap[1]:
        wait_send(item)
    to_sib.wait_send()
    to_rest.wait_send()


def shards(state, coefs, lagged_absorbers, sun_route, band_coef, solar, layer_mass, remap_index, remap_weight):
    sizes = tuple(lax.axis_size(a) for a in ("grp", "gx", "gy"))
    chips = sizes[0] // 2
    gases = lagged_absorbers.shape[0]
    levels, rows = state.shape[1:3]
    f32, bf16, i16 = jnp.float32, jnp.bfloat16, jnp.int16
    operands = (
        state, coefs, lagged_absorbers, sun_route.T, band_coef.T, solar.reshape(1, -1), layer_mass.reshape(1, -1),
        remap_index.T, remap_weight.T,
    )
    n_copies = 16 + 1 + (chips - 1) + 1 + 2
    return pl.pallas_call(
        functools.partial(kernel, sizes),
        out_shape=(jax.ShapeDtypeStruct(state.shape, f32), jax.ShapeDtypeStruct(state.shape[1:], f32)),
        in_specs=[pl.BlockSpec(memory_space=pltpu.HBM)] * len(operands),
        out_specs=(pl.BlockSpec(memory_space=pltpu.VMEM),) * 2,
        scratch_shapes=[
            pltpu.VMEM((1, rows), jnp.int32),
            pltpu.VMEM(band_coef.shape[::-1], bf16),
            pltpu.VMEM((1, solar.shape[0]), f32),
            pltpu.SMEM((1, layer_mass.shape[0]), f32),
            pltpu.SMEM(remap_index.shape[::-1], jnp.int32),
            pltpu.SMEM(remap_weight.shape[::-1], f32),
            pltpu.VMEM((5, 2 * levels * (rows + 2 * H), 128), f32),
            pltpu.VMEM(lagged_absorbers.shape, bf16),
            pltpu.VMEM((PLANES, rows, 128), i16),
            pltpu.VMEM((2, PLANES, H, 128), i16),
            pltpu.VMEM((2, 3, rows + 16, 128), i16),
            pltpu.VMEM((2, 3, rows + 16, 128), i16),
            pltpu.VMEM((2, 3, rows, 128), bf16),
            pltpu.VMEM((2, 2, 3, H, 128), bf16),
            pltpu.VMEM((32, 128), f32),
            pltpu.VMEM((2, 3, levels * rows, 128), f32),
            pltpu.VMEM((2, 2, 3, RIM * rows // 2, 128), f32),
            pltpu.VMEM((PLANES - DIRECT, H, 128), i16),
            *[pltpu.VMEM((rows // 2 + 2 * H, 2 * levels, 128), f32)] * 6,
            pltpu.VMEM((gases, rows, 128), f32),
            pltpu.VMEM((gases, rows // 2, 128), f32),
            pltpu.VMEM((gases, rows // 2, 128), i16),
            pltpu.VMEM((chips - 1, gases, rows // 2, 128), i16),
            pltpu.VMEM((gases, rows // 2, 128), f32),
            pltpu.VMEM((gases, rows // 2, 128), f32),
            pltpu.VMEM((gases, rows // 2, 128), f32),
            pltpu.VMEM((8 * band_coef.shape[0], 128), bf16),
            pltpu.VMEM((rows, 128), f32),
            pltpu.SemaphoreType.DMA((2, levels)),
            pltpu.SemaphoreType.DMA((7,)),
            pltpu.SemaphoreType.DMA((n_copies,)),
            pltpu.SemaphoreType.DMA((n_copies,)),
            pltpu.SemaphoreType.REGULAR((4,)),
        ],
        compiler_params=pltpu.CompilerParams(collective_id=0, has_side_effects=True, vmem_limit_bytes=40 * 2**20),
    )(
        *[pltpu.with_memory_space_constraint(a, pltpu.HBM) for a in operands]
    )


def solution(mesh):
    tiles = P(None, "grp", "gy", "gx")
    in_specs = (tiles, tiles, tiles, P("gy", "gx"), P(), P(), P(), P(), P())
    out_specs = (tiles, P("grp", "gy", "gx"))
    return jax.shard_map(shards, mesh=mesh, in_specs=in_specs, out_specs=out_specs, check_vma=False)
```

```python
import functools

import jax
import jax.numpy as jnp
from jax import lax
from jax.experimental import pallas as pl
from jax.experimental.pallas import tpu as pltpu
from jax.sharding import PartitionSpec as P

SUB = 8
RIM = 2
H = 2 * SUB
NDARK = 16
PLANES = 22
DIRECT = 10
MESH = pl.DeviceIdType.MESH
LOG2E = 1.4426950408889634


def encode(values, biggest):
    return jnp.round(values * (32700.0 * jnp.exp2(-biggest))).astype(jnp.int32).astype(jnp.int16)


def decode(codes, biggest):
    return codes.astype(jnp.int32).astype(jnp.float32) * (jnp.exp2(biggest) * (1.0 / 32700.0))


def exponent(values):
    top = jnp.max(jnp.abs(values), axis=0, keepdims=True)
    return jnp.ceil(jnp.log2(jnp.maximum(top, 1e-30)) + 1e-3)


def lane_ids(rows):
    return lax.broadcasted_iota(jnp.int32, (rows, 128), 1)


def turned(v, shift):
    lane = lax.broadcasted_iota(jnp.int32, v.shape, 2)
    same = pltpu.roll(v, shift % 128, 2)
    across = pltpu.roll(same, 4, 1)
    keep = lane >= shift if shift > 0 else lane < 128 + shift
    return jnp.where(keep, same, across)


def chunks(start, stop, size=8):
    return [(i, min(i + size, stop)) for i in range(start, stop, size)]


def prepare(wide, base, start, stop, p, fx, fy, bx, by, st):
    tall_rows = wide.shape[1] // 8

    def row(c, r):
        return wide[c, pl.ds(base + r, 8, stride=tall_rows), :]

    for i, j in chunks(start, stop):
        for r in range(i, j):
            p[r] = row(2, r)
            st[r] = row(4, r)
            if r > 0:
                fx[r - 1] = row(0, r)
                bx[r - 1] = row(3, r)
        fy[i:j] = turned(jnp.stack([row(1, r) for r in range(i, j)]), -1)
        by[i:j] = turned(jnp.stack([row(3, r) for r in range(i, j)]), -1)


def substeps(p, fx, fy, bx, by, st, out):
    rows = p.shape[0]
    first = 0
    pv, xv, yv = p[...], fx[0 : rows - 1], fy[...]
    for step in range(SUB):
        n = rows - 2 * first
        xv = xv[0 : n - 2] - bx[first : first + n - 2] * (pv[2:n] - pv[0 : n - 2])
        here = pv[2 : n - 2]
        inner = slice(first + 2, first + n - 2)
        yv = yv[2 : n - 2] - by[inner] * (turned(here, -2) - here)
        across = yv - turned(yv, 2)
        pv = here - st[inner] * ((xv[2 : n - 2] - xv[0 : n - 4]) + across)
        last, xv = xv, xv[2 : n - 2]
        first += 2
    own = rows - 2 * H
    moved = turned(yv, 1)
    for r in range(own):
        out[0, pl.ds(r, 8, stride=own), :] = last[r + 1]
        out[1, pl.ds(r, 8, stride=own), :] = moved[r]
        out[2, pl.ds(r, 8, stride=own), :] = pv[r]


def kernel(
    sizes,
    state, coefs, absorbers, route_row, band_rows, solar_row, mass_row, ridx_rows, rweight_rows,
    new_state, heating,
    route, band, solar, mass, ridx, rweight,
    wide, gas, rows_out, rows_in, sides_out, sides_in, corners_out, corners_in, exps, out, near, passing,
    p, fx, fy, bx, by, st, block_sum, sib, chip_sum, lower, part, rest, prefix, lhs, sunlit,
    tile_sem, in_sem, send_sem, recv_sem, ready,
):
    n_grp, n_gx, n_gy = sizes
    dyn_groups = 3 * n_grp // 4
    chips = n_grp // 2
    levels, rows = 4, 32
    me, gx, gy = lax.axis_index("grp"), lax.axis_index("gx"), lax.axis_index("gy")
    core, chip = lax.rem(me, 2), lax.div(me, 2)
    dyn = me < dyn_groups
    has_l, has_r = gx > 0, gx < n_gx - 1
    has_u, has_d = gy > 0, gy < n_gy - 1
    land = jnp.logical_and

    loads = [
        pltpu.make_async_copy(absorbers, gas, in_sem.at[0]),
        pltpu.make_async_copy(band_rows, band, in_sem.at[1]),
        pltpu.make_async_copy(solar_row, solar, in_sem.at[2]),
        pltpu.make_async_copy(route_row, route, in_sem.at[3]),
        pltpu.make_async_copy(ridx_rows, ridx, in_sem.at[4]),
        pltpu.make_async_copy(rweight_rows, rweight, in_sem.at[5]),
        pltpu.make_async_copy(mass_row, mass, in_sem.at[6]),
    ]
    tall_rows = rows + 2 * H
    tiles = []
    for l in range(levels):
        at = tall_rows * l + H
        tiles.append(pltpu.make_async_copy(state.at[:, l], wide.at[0:3, at : at + rows, :], tile_sem.at[0, l]))
        tiles.append(pltpu.make_async_copy(coefs.at[:, l], wide.at[3:5, at : at + rows, :], tile_sem.at[1, l]))
    for load in tiles:
        load.start()

    seam = n_gy // 2
    far = seam >= 2
    edge_d, edge_u = land(dyn, gy == seam - 1), land(dyn, gy == seam)
    first = me < 2
    pass_d = land(dyn, jnp.where(gy == seam - 1, me + 2 < dyn_groups, land(gy == seam - 2, first)))
    by_way = {"grp": jnp.where(first, me, me - 2), "gy": jnp.where(first, seam - 2, seam - 1)}
    beyond = {"grp": jnp.where(gy == seam - 1, me + 2, me), "gy": seam + 0 * gy}
    above_us, below_us = [], []
    for dx, cx in ((0, True), (-1, has_l), (1, has_r)):
        here = land(dyn, cx)
        above_us.append((land(here, has_u), {"gx": gx + dx, "gy": gy - 1}))
        below_us.append((land(here, has_d), {"gx": gx + dx, "gy": gy + 1}))
    aside = [
        (land(dyn, has_r), gx + 1 <= n_gx // 2, {"gx": gx + 1}),
        (land(dyn, has_l), gx - 1 >= n_gx // 2, {"gx": gx - 1}),
    ]
    same_tile = []
    for d in sorted({1} | {2 * d for d in range(1, chips)}):
        for other_me, cond in ((me + d, me + d < n_grp), (me - d, me - d >= 0)):
            other_chip = lax.div(jnp.maximum(other_me, 0), 2)
            farther = jnp.where(gy < seam, other_chip > chip, other_chip < chip)
            late = jnp.where(other_chip == chip, core == 1, farther)
            same_tile.append((cond, late, {"grp": other_me}))
    beside = aside + same_tile
    barrier = pltpu.get_barrier_semaphore()

    def signal(sem, cond, dev):
        @pl.when(cond)
        def _():
            pl.semaphore_signal(sem, inc=1, device_id=dev, device_id_type=MESH)

    def number_of(conds):
        return functools.reduce(lambda n, c: n + c.astype(jnp.int32), conds, jnp.int32(0))

    below_late, above_late = ~edge_d, edge_u
    for cond, dev in below_us:
        signal(barrier, land(cond, below_late), dev)
    for cond, dev in above_us:
        signal(barrier, land(cond, above_late), dev)
    for cond, late, dev in beside:
        signal(barrier, land(cond, late), dev)
    for load in loads:
        load.start()
    count = number_of([land(cond, ~late) for cond, late, _ in beside])
    count = count + number_of([land(cond, ~above_late) for cond, _ in above_us]) + number_of([land(cond, ~below_late) for cond, _ in below_us])
    if far:
        signal(barrier, edge_u, by_way)
        count = count + pass_d.astype(jnp.int32)

    number = [0]

    def remote(src, dst, dev, arrival=None):
        i = number[0]
        number[0] += 1
        return pltpu.make_async_remote_copy(
            src_ref=src,
            dst_ref=dst,
            send_sem=send_sem.at[i],
            recv_sem=recv_sem.at[i if arrival is None else arrival],
            device_id=dev,
            device_id_type=MESH,
        )

    def all_of(*conds):
        return functools.reduce(land, conds)

    down, up = all_of(dyn, has_d), all_of(dyn, has_u)
    rest_down = rows_out.at[DIRECT:PLANES, rows - H :]
    rest_up = rows_out.at[DIRECT:PLANES, 0:H]
    down_sem = number[0]
    by_down = (land(down, ~edge_d) if far else down, up, remote(rest_down, rows_in.at[0, DIRECT:PLANES], {"gy": gy + 1}))
    to_below = [(down, up, remote(rows_out.at[0:DIRECT, rows - H :], rows_in.at[0, 0:DIRECT], {"gy": gy + 1})), by_down]
    to_above = [
        (up, down, remote(rows_out.at[0:DIRECT, 0:H], rows_in.at[1, 0:DIRECT], {"gy": gy - 1})),
        (up, down, remote(rest_up, rows_in.at[1, DIRECT:PLANES], {"gy": gy - 1})),
    ]
    passes, relays = [], []
    if far:
        passes = [(edge_d, pass_d, remote(rest_down, passing, by_way))]
        relays = [(pass_d, None, remote(passing, rows_in.at[0, DIRECT:PLANES], beyond, down_sem))]
    to_sides = [
        (all_of(dyn, has_r), all_of(dyn, has_l), remote(sides_out.at[0], sides_in.at[0], {"gx": gx + 1})),
        (all_of(dyn, has_l), all_of(dyn, has_r), remote(sides_out.at[1], sides_in.at[1], {"gx": gx - 1})),
    ]
    for side, (to, back, dx) in enumerate(((has_r, has_l, 1), (has_l, has_r, -1))):
        bottom = corners_out.at[side, :, rows - H :]
        top = corners_out.at[side, :, 0:H]
        to_below.append(
            (all_of(dyn, to, has_d), all_of(dyn, back, has_u), remote(bottom, corners_in.at[side, 0], {"gx": gx + dx, "gy": gy + 1}))
        )
        to_above.append(
            (all_of(dyn, to, has_u), all_of(dyn, back, has_d), remote(top, corners_in.at[side, 1], {"gx": gx + dx, "gy": gy - 1}))
        )
    halo = to_below + to_above + to_sides
    half = rows // 2
    mine = pl.multiple_of(half * core, half)
    other = pl.multiple_of(half * (1 - core), half)
    sibling = {"grp": me + 1 - 2 * core}
    to_sib = remote(block_sum.at[:, pl.ds(other, half)], sib, sibling)
    to_chips = [
        (chip + d < chips, chip - d >= 0, remote(chip_sum, lower.at[d - 1], {"grp": me + 2 * d})) for d in range(1, chips)
    ]
    to_rest = remote(part, rest, sibling)
    remap = [
        [
            (me > 0, me < n_grp - 1, remote(out.at[h, :, 0 : RIM * half], near.at[1, h], {"grp": me - 1})),
            (me < n_grp - 1, me > 0, remote(out.at[h, :, (levels - RIM) * half : levels * half], near.at[0, h], {"grp": me + 1})),
        ]
        for h in range(2)
    ]

    def start(item, when=None):
        @pl.when(item[0] if when is None else land(item[0], when))
        def _():
            item[2].start()

    def wait_recv(item):
        @pl.when(item[1])
        def _():
            item[2].wait_recv()

    def wait_send(item):
        @pl.when(item[0])
        def _():
            item[2].wait_send()

    @pl.when(count > 0)
    def _():
        pl.semaphore_wait(barrier, count)

    for cond, dev in above_us:
        signal(ready.at[0], land(cond, ~above_late), dev)
    for cond, dev in below_us:
        signal(ready.at[1], land(cond, ~below_late), dev)
    for cond, late, dev in aside:
        signal(ready.at[2], land(cond, ~late), dev)
    for cond, late, dev in same_tile:
        signal(ready.at[3], land(cond, ~late), dev)

    def await_ready(i, conds):
        n = number_of(conds)

        @pl.when(n > 0)
        def _():
            pl.semaphore_wait(ready.at[i], n)


    exps[...] = jnp.zeros(exps.shape, jnp.float32)
    for l in range(levels):
        for load in tiles[2 * l : 2 * l + 2]:
            load.wait()
        for c in range(5):
            cells = wide[c, tall_rows * l + H : tall_rows * l + H + rows, :]
            biggest = exponent(cells)
            exps[levels * c + l : levels * c + l + 1, :] = biggest
            rows_out[levels * c + l] = encode(cells, biggest)
    for i in range(2):
        held = exps[16 * i : 16 * i + 16, :]
        rows_out[20 + i] = jnp.concatenate([held, held], axis=0).astype(jnp.int32).astype(jnp.int16)

    for item in passes:
        start(item)
    for item in to_below[:2]:
        start(item, ~below_late)
    for item in to_above[:2]:
        start(item, ~above_late)

    lane = lane_ids(rows)
    for q in range(3):
        right = jnp.zeros((rows, 128), jnp.float32)
        left = jnp.zeros((rows, 128), jnp.float32)
        for c in (2 * q, 2 * q + 1):
            if c > 4:
                continue
            for l in range(levels):
                t = 2 * l + c % 2
                cells = wide[c, tall_rows * l + H : tall_rows * l + H + rows, :]
                here = lax.div(lane, 16) == t
                shift = (16 * t + 16) % 128
                right = jnp.where(here, pltpu.roll(cells, shift, 1) if shift else cells, right)
                shift = 16 * t
                left = jnp.where(here, pltpu.roll(cells, shift, 1) if shift else cells, left)
        for side, strip in enumerate((right, left)):
            biggest = exponent(strip)
            sides_out[side, q, 0:rows] = encode(strip, biggest)
            sides_out[side, q, rows : rows + 16] = jnp.broadcast_to(biggest, (16, 128)).astype(jnp.int32).astype(jnp.int16)
            corners_out[side, q] = strip.astype(jnp.bfloat16)

    for item in to_below[2:]:
        start(item, ~below_late)
    for item in to_above[2:]:
        start(item, ~above_late)
    for item, relay in zip(passes, relays):
        wait_recv(item)
        start(relay)
    await_ready(2, [land(cond, late) for cond, late, _ in aside])
    for item in to_sides:
        start(item)

    loads[0].wait()
    for f in range(gas.shape[0]):
        total = gas[f, 0].astype(jnp.float32)
        for l in range(1, levels):
            total = total + gas[f, l].astype(jnp.float32)
        block_sum[f] = total
    await_ready(3, [land(cond, late) for cond, late, _ in same_tile])
    to_sib.start()

    await_ready(0, [land(cond, below_late) for cond, _ in below_us])
    for item in to_below:
        start(item, below_late)

    def fill(cond, ref, *index, value=0):
        @pl.when(cond)
        def _():
            view = ref.at[index] if index else ref
            view[...] = jnp.full(view.shape, value, view.dtype)

    fill(~has_u, rows_in, 0)
    fill(~has_d, rows_in, 1)
    fill(~has_l, sides_in, 0)
    fill(~has_r, sides_in, 1)
    fill(~land(has_l, has_u), corners_in, 0, 0)
    fill(~land(has_l, has_d), corners_in, 0, 1)
    fill(~land(has_r, has_u), corners_in, 1, 0)
    fill(~land(has_r, has_d), corners_in, 1, 1)
    fill(me == 0, near, 0)
    fill(me == n_grp - 1, near, 1)
    for d in range(1, chips):
        fill(chip - d < 0, lower, d - 1, value=-4 * 8191)

    @pl.when(~dyn)
    def _():
        for c in range(3):
            for l in range(levels):
                for h in range(2):
                    at = tall_rows * l + H + half * h
                    out[h, c, half * l : half * l + half, :] = wide[c, at : at + half, :]

    for load in loads[1:]:
        load.wait()
    gases, gpoints = band.shape
    r0 = lax.broadcasted_iota(jnp.int32, (gpoints, gpoints), 0)
    r1 = lax.broadcasted_iota(jnp.int32, (gpoints, gpoints), 1)
    logs = jnp.log2(solar[...])
    high = logs.astype(jnp.bfloat16).astype(jnp.float32)
    middle = (logs - high).astype(jnp.bfloat16).astype(jnp.float32)
    low = logs - high - middle
    srcs = jnp.concatenate([band[...].astype(jnp.float32), high, middle, low], axis=0).astype(jnp.bfloat16)
    n_src = gases + 3
    l0 = lax.broadcasted_iota(jnp.int32, (rows, rows), 0)
    l1 = lax.broadcasted_iota(jnp.int32, (rows, rows), 1)
    lit_row = jnp.broadcast_to((route[...] < NDARK).astype(jnp.float32), (rows, rows))
    sunlit[...] = jnp.broadcast_to(jnp.sum(jnp.where(l0 == l1, lit_row, 0.0), axis=1, keepdims=True), (rows, 128))
    spread0 = lax.div(lax.broadcasted_iota(jnp.int32, (8 * gpoints, gpoints), 0), 8)
    spread1 = lax.broadcasted_iota(jnp.int32, (8 * gpoints, gpoints), 1)
    spread = (spread0 == spread1).astype(jnp.float32).astype(jnp.bfloat16)
    tall = lax.dot_general(spread, srcs, (((1,), (1,)), ((), ())), preferred_element_type=jnp.float32).astype(jnp.bfloat16)
    w0 = lax.broadcasted_iota(jnp.int32, (n_src, 128), 0)
    w1 = lax.broadcasted_iota(jnp.int32, (n_src, 128), 1)
    in_gas = w1 < 16 * gases
    owner = jnp.where(in_gas, lax.rem(lax.div(w1, 8), gases), w1 - 16 * gases + gases)
    widen = (w0 == owner).astype(jnp.float32).astype(jnp.bfloat16)
    spread_all = jnp.dot(tall, widen, preferred_element_type=jnp.float32)
    m0 = lax.broadcasted_iota(jnp.int32, (8 * gpoints, 128), 0)
    m1 = lax.broadcasted_iota(jnp.int32, (8 * gpoints, 128), 1)
    keep = (m1 >= 16 * gases) | (lax.rem(m0, 8) == lax.rem(m1, 8))
    lhs[...] = jnp.where(keep, spread_all, 0.0).astype(jnp.bfloat16)

    to_sib.wait_recv()
    both = block_sum[:, pl.ds(mine, half), :] + sib[...]
    chip_sum[...] = jnp.round((both - 4.0) * 8191.0).astype(jnp.int32).astype(jnp.int16)
    for item in to_chips:
        start(item)

    def radiate(start_row, ref):
        columns = []
        for g in range(half // 8):
            depth = ref[:, 8 * g : 8 * g + 8, :]
            for l in range(levels + 1):
                if l:
                    cells = gas[:, l - 1, pl.ds(start_row, half), :].astype(jnp.float32)
                    depth = depth + cells[:, 8 * g : 8 * g + 8, :]
                scaled = (depth * -LOG2E).reshape(8 * gases, 128)
                high = scaled.astype(jnp.bfloat16).astype(jnp.float32)
                stack = jnp.concatenate([high, scaled - high, jnp.ones((128 - 16 * gases, 128), jnp.float32)], axis=0)
                columns.append(stack.astype(jnp.bfloat16))
        cols = jnp.concatenate(columns, axis=1)
        expo = jnp.dot(lhs[...], cols, preferred_element_type=jnp.float32)
        flux = jnp.sum(jnp.exp2(expo).reshape(gpoints, 8, cols.shape[1]), axis=0)
        for l in range(levels):
            parts = []
            for g in range(half // 8):
                at = 128 * (g * (levels + 1) + l)
                parts.append(flux[:, at : at + 128] - flux[:, at + 128 : at + 256])
            diff = jnp.concatenate(parts, axis=0)
            lit = sunlit[pl.ds(start_row, half), :] > 0.5
            rate = diff / jnp.full((half, 128), mass[0, levels * me + l])
            heating[l, pl.ds(start_row, half), :] = jnp.where(lit, rate, 0.0)

    def shine():
        for item in to_chips:
            wait_recv(item)
        above = jnp.zeros(rest.shape, jnp.float32)
        for d in range(1, chips):
            above = above + (lower[d - 1].astype(jnp.int32).astype(jnp.float32) * (1.0 / 8191.0) + 4.0)
        even = (core == 0).astype(jnp.float32)
        part[...] = above + even * block_sum[:, pl.ds(mine, half), :]
        to_rest.start()
        prefix[...] = above + (1.0 - even) * sib[...]
        radiate(mine, prefix)
        to_rest.wait_recv()
        radiate(other, rest)

    waits = land(gy >= seam - 1, gy <= seam)

    @pl.when(waits)
    def _():
        shine()

    lane_h = lane_ids(rows + H)

    def decode_rows(i, at):
        exps[...] = jnp.concatenate([rows_in[i, 20], rows_in[i, 21]], axis=0).astype(jnp.int32).astype(jnp.float32)
        for c in range(5):
            for l in range(levels):
                k = levels * c + l
                wide[c, tall_rows * l + at : tall_rows * l + at + H, :] = decode(rows_in[i, k], exps[k : k + 1, :])

    def place_sides(q, strips, at):
        n = strips[0].shape[0]
        for c in (2 * q, 2 * q + 1):
            if c > 4:
                continue
            for l in range(levels):
                t = 2 * l + c % 2
                shift = (112 - 16 * t) % 128
                left = pltpu.roll(strips[0], shift, 1) if shift else strips[0]
                shift = (128 - 16 * t) % 128
                right = pltpu.roll(strips[1], shift, 1) if shift else strips[1]
                start_row = tall_rows * (levels + l) + at
                wide[c, start_row : start_row + n, :] = jnp.where(
                    lane_h[0:n] < 16, right, jnp.where(lane_h[0:n] >= 112, left, 0.0)
                )

    for item in to_above + to_sides:
        wait_recv(item)

    @pl.when(dyn)
    def _():
        decode_rows(1, H + rows)
        for q in range(3):
            strips = []
            for side in range(2):
                biggest = sides_in[side, q, rows : rows + 16].astype(jnp.int32).astype(jnp.float32)[0:1]
                middle = decode(sides_in[side, q, 0:rows], biggest)
                strips.append(jnp.concatenate([middle, corners_in[side, 1, q].astype(jnp.float32)], axis=0))
            place_sides(q, strips, H)
        prepare(wide, half, 0, half + 2 * H, p, fx, fy, bx, by, st)
        substeps(p, fx, fy, bx, by, st, out.at[1])

    for item in remap[1]:
        start(item)
    await_ready(1, [land(cond, above_late) for cond, _ in above_us])
    for item in to_above:
        start(item, above_late)

    @pl.when(dyn)
    def _():
        prepare(wide, 0, H, half + 2 * H, p, fx, fy, bx, by, st)

    for item in to_below:
        wait_recv(item)

    @pl.when(dyn)
    def _():
        decode_rows(0, 0)
        for q in range(3):
            place_sides(q, [corners_in[side, 0, q].astype(jnp.float32) for side in range(2)], 0)
        prepare(wide, 0, 0, H, p, fx, fy, bx, by, st)
        substeps(p, fx, fy, bx, by, st, out.at[0])

    for item in remap[0]:
        start(item)

    @pl.when(~waits)
    def _():
        shine()

    weights = []
    for kl in range(levels):
        k = levels * me + kl
        for o in range(-RIM, RIM + 1):
            w = jnp.float32(0)
            for j in range(ridx.shape[0]):
                w = w + jnp.where(ridx[j, k] == k + o, rweight[j, k], jnp.float32(0))
            weights.append(w)
    for h in (1, 0):
        for item in remap[h]:
            wait_recv(item)
        for kl in range(levels):
            for c in range(3):
                acc = jnp.zeros((half, 128), jnp.float32)
                for o in range(-RIM, RIM + 1):
                    m = kl + o
                    if m < 0:
                        cells = near[0, h, c, half * (m + RIM) : half * (m + RIM + 1), :]
                    elif m < levels:
                        cells = out[h, c, half * m : half * m + half, :]
                    else:
                        cells = near[1, h, c, half * (m - levels) : half * (m - levels + 1), :]
                    acc = acc + weights[(2 * RIM + 1) * kl + o + RIM] * cells
                new_state[c, kl, half * h : half * h + half, :] = acc

    for item in passes + relays + halo + to_chips + remap[0] + remap[1]:
        wait_send(item)
    to_sib.wait_send()
    to_rest.wait_send()


def shards(state, coefs, lagged_absorbers, sun_route, band_coef, solar, layer_mass, remap_index, remap_weight):
    sizes = tuple(lax.axis_size(a) for a in ("grp", "gx", "gy"))
    chips = sizes[0] // 2
    gases = lagged_absorbers.shape[0]
    levels, rows = state.shape[1:3]
    f32, bf16, i16 = jnp.float32, jnp.bfloat16, jnp.int16
    operands = (
        state, coefs, lagged_absorbers, sun_route.T, band_coef.T, solar.reshape(1, -1), layer_mass.reshape(1, -1),
        remap_index.T, remap_weight.T,
    )
    n_copies = 16 + 1 + (chips - 1) + 1 + 2
    return pl.pallas_call(
        functools.partial(kernel, sizes),
        out_shape=(jax.ShapeDtypeStruct(state.shape, f32), jax.ShapeDtypeStruct(state.shape[1:], f32)),
        in_specs=[pl.BlockSpec(memory_space=pltpu.HBM)] * len(operands),
        out_specs=(pl.BlockSpec(memory_space=pltpu.VMEM),) * 2,
        scratch_shapes=[
            pltpu.VMEM((1, rows), jnp.int32),
            pltpu.VMEM(band_coef.shape[::-1], bf16),
            pltpu.VMEM((1, solar.shape[0]), f32),
            pltpu.SMEM((1, layer_mass.shape[0]), f32),
            pltpu.SMEM(remap_index.shape[::-1], jnp.int32),
            pltpu.SMEM(remap_weight.shape[::-1], f32),
            pltpu.VMEM((5, 2 * levels * (rows + 2 * H), 128), f32),
            pltpu.VMEM(lagged_absorbers.shape, bf16),
            pltpu.VMEM((PLANES, rows, 128), i16),
            pltpu.VMEM((2, PLANES, H, 128), i16),
            pltpu.VMEM((2, 3, rows + 16, 128), i16),
            pltpu.VMEM((2, 3, rows + 16, 128), i16),
            pltpu.VMEM((2, 3, rows, 128), bf16),
            pltpu.VMEM((2, 2, 3, H, 128), bf16),
            pltpu.VMEM((32, 128), f32),
            pltpu.VMEM((2, 3, levels * rows, 128), f32),
            pltpu.VMEM((2, 2, 3, RIM * rows // 2, 128), f32),
            pltpu.VMEM((PLANES - DIRECT, H, 128), i16),
            *[pltpu.VMEM((rows // 2 + 2 * H, 2 * levels, 128), f32)] * 6,
            pltpu.VMEM((gases, rows, 128), f32),
            pltpu.VMEM((gases, rows // 2, 128), f32),
            pltpu.VMEM((gases, rows // 2, 128), i16),
            pltpu.VMEM((chips - 1, gases, rows // 2, 128), i16),
            pltpu.VMEM((gases, rows // 2, 128), f32),
            pltpu.VMEM((gases, rows // 2, 128), f32),
            pltpu.VMEM((gases, rows // 2, 128), f32),
            pltpu.VMEM((8 * band_coef.shape[0], 128), bf16),
            pltpu.VMEM((rows, 128), f32),
            pltpu.SemaphoreType.DMA((2, levels)),
            pltpu.SemaphoreType.DMA((7,)),
            pltpu.SemaphoreType.DMA((n_copies,)),
            pltpu.SemaphoreType.DMA((n_copies,)),
            pltpu.SemaphoreType.REGULAR((4,)),
        ],
        compiler_params=pltpu.CompilerParams(collective_id=0, has_side_effects=True, vmem_limit_bytes=40 * 2**20),
    )(
        *[pltpu.with_memory_space_constraint(a, pltpu.HBM) for a in operands]
    )


def solution(mesh):
    tiles = P(None, "grp", "gy", "gx")
    in_specs = (tiles, tiles, tiles, P("gy", "gx"), P(), P(), P(), P(), P())
    out_specs = (tiles, P("grp", "gy", "gx"))
    return jax.shard_map(shards, mesh=mesh, in_specs=in_specs, out_specs=out_specs, check_vma=False)
```

```python
import functools

import jax
import jax.numpy as jnp
from jax import lax
from jax.experimental import pallas as pl
from jax.experimental.pallas import tpu as pltpu
from jax.sharding import PartitionSpec as P

SUB = 8
RIM = 2
H = 2 * SUB
NDARK = 16
PLANES = 22
DIRECT = 10
MESH = pl.DeviceIdType.MESH
LOG2E = 1.4426950408889634


def encode(values, biggest):
    return jnp.round(values * (32700.0 * jnp.exp2(-biggest))).astype(jnp.int32).astype(jnp.int16)


def decode(codes, biggest):
    return codes.astype(jnp.int32).astype(jnp.float32) * (jnp.exp2(biggest) * (1.0 / 32700.0))


def exponent(values):
    top = jnp.max(jnp.abs(values), axis=0, keepdims=True)
    return jnp.ceil(jnp.log2(jnp.maximum(top, 1e-30)) + 1e-3)


def lane_ids(rows):
    return lax.broadcasted_iota(jnp.int32, (rows, 128), 1)


def turned(v, shift):
    lane = lax.broadcasted_iota(jnp.int32, v.shape, 2)
    same = pltpu.roll(v, shift % 128, 2)
    across = pltpu.roll(same, 4, 1)
    keep = lane >= shift if shift > 0 else lane < 128 + shift
    return jnp.where(keep, same, across)


def chunks(start, stop, size=8):
    return [(i, min(i + size, stop)) for i in range(start, stop, size)]


def prepare(wide, base, start, stop, p, fx, fy, bx, by, st):
    tall_rows = wide.shape[1] // 8

    def row(c, r):
        return wide[c, pl.ds(base + r, 8, stride=tall_rows), :]

    for i, j in chunks(start, stop):
        for r in range(i, j):
            p[r] = row(2, r)
            st[r] = row(4, r)
            if r > 0:
                fx[r - 1] = row(0, r)
                bx[r - 1] = row(3, r)
        fy[i:j] = turned(jnp.stack([row(1, r) for r in range(i, j)]), -1)
        by[i:j] = turned(jnp.stack([row(3, r) for r in range(i, j)]), -1)


def substeps(p, fx, fy, bx, by, st, out):
    rows = p.shape[0]
    first = 0
    pv, xv, yv = p[...], fx[0 : rows - 1], fy[...]
    for step in range(SUB):
        n = rows - 2 * first
        xv = xv[0 : n - 2] - bx[first : first + n - 2] * (pv[2:n] - pv[0 : n - 2])
        here = pv[2 : n - 2]
        inner = slice(first + 2, first + n - 2)
        yv = yv[2 : n - 2] - by[inner] * (turned(here, -2) - here)
        across = yv - turned(yv, 2)
        pv = here - st[inner] * ((xv[2 : n - 2] - xv[0 : n - 4]) + across)
        last, xv = xv, xv[2 : n - 2]
        first += 2
    own = rows - 2 * H
    moved = turned(yv, 1)
    for r in range(own):
        out[0, pl.ds(r, 8, stride=own), :] = last[r + 1]
        out[1, pl.ds(r, 8, stride=own), :] = moved[r]
        out[2, pl.ds(r, 8, stride=own), :] = pv[r]


def kernel(
    sizes,
    state, coefs, absorbers, route_row, band_rows, solar_row, mass_row, ridx_rows, rweight_rows,
    new_state, heating,
    route, band, solar, mass, ridx, rweight,
    wide, gas, rows_out, rows_in, sides_out, sides_in, corners_out, corners_in, exps, out, near, passing,
    p, fx, fy, bx, by, st, block_sum, sib, chip_sum, lower, part, rest, prefix, lhs, sunlit,
    tile_sem, in_sem, send_sem, recv_sem, ready,
):
    n_grp, n_gx, n_gy = sizes
    dyn_groups = 3 * n_grp // 4
    chips = n_grp // 2
    levels, rows = 4, 32
    me, gx, gy = lax.axis_index("grp"), lax.axis_index("gx"), lax.axis_index("gy")
    core, chip = lax.rem(me, 2), lax.div(me, 2)
    dyn = me < dyn_groups
    has_l, has_r = gx > 0, gx < n_gx - 1
    has_u, has_d = gy > 0, gy < n_gy - 1
    land = jnp.logical_and

    loads = [
        pltpu.make_async_copy(absorbers, gas, in_sem.at[0]),
        pltpu.make_async_copy(band_rows, band, in_sem.at[1]),
        pltpu.make_async_copy(solar_row, solar, in_sem.at[2]),
        pltpu.make_async_copy(route_row, route, in_sem.at[3]),
        pltpu.make_async_copy(ridx_rows, ridx, in_sem.at[4]),
        pltpu.make_async_copy(rweight_rows, rweight, in_sem.at[5]),
        pltpu.make_async_copy(mass_row, mass, in_sem.at[6]),
    ]
    tall_rows = rows + 2 * H
    tiles = []
    for l in range(levels):
        at = tall_rows * l + H
        tiles.append(pltpu.make_async_copy(state.at[:, l], wide.at[0:3, at : at + rows, :], tile_sem.at[0, l]))
        tiles.append(pltpu.make_async_copy(coefs.at[:, l], wide.at[3:5, at : at + rows, :], tile_sem.at[1, l]))
    for load in tiles:
        load.start()

    seam = n_gy // 2
    far = seam >= 2
    edge_d, edge_u = land(dyn, gy == seam - 1), land(dyn, gy == seam)
    first = me < 2
    pass_d = land(dyn, jnp.where(gy == seam - 1, me + 2 < dyn_groups, land(gy == seam - 2, first)))
    by_way = {"grp": jnp.where(first, me, me - 2), "gy": jnp.where(first, seam - 2, seam - 1)}
    beyond = {"grp": jnp.where(gy == seam - 1, me + 2, me), "gy": seam + 0 * gy}
    above_us, below_us = [], []
    for dx, cx in ((0, True), (-1, has_l), (1, has_r)):
        here = land(dyn, cx)
        above_us.append((land(here, has_u), {"gx": gx + dx, "gy": gy - 1}))
        below_us.append((land(here, has_d), {"gx": gx + dx, "gy": gy + 1}))
    aside = [
        (land(dyn, has_r), gx + 1 <= n_gx // 2, {"gx": gx + 1}),
        (land(dyn, has_l), gx - 1 >= n_gx // 2, {"gx": gx - 1}),
    ]
    same_tile = []
    for d in sorted({1} | {2 * d for d in range(1, chips)}):
        for other_me, cond in ((me + d, me + d < n_grp), (me - d, me - d >= 0)):
            other_chip = lax.div(jnp.maximum(other_me, 0), 2)
            farther = jnp.where(gy < seam, other_chip > chip, other_chip < chip)
            late = jnp.where(other_chip == chip, core == 1, farther)
            same_tile.append((cond, late, {"grp": other_me}))
    beside = aside + same_tile
    barrier = pltpu.get_barrier_semaphore()

    def signal(sem, cond, dev):
        @pl.when(cond)
        def _():
            pl.semaphore_signal(sem, inc=1, device_id=dev, device_id_type=MESH)

    def number_of(conds):
        return functools.reduce(lambda n, c: n + c.astype(jnp.int32), conds, jnp.int32(0))

    below_late, above_late = ~edge_d, edge_u
    for cond, dev in below_us:
        signal(barrier, land(cond, below_late), dev)
    for cond, dev in above_us:
        signal(barrier, land(cond, above_late), dev)
    for cond, late, dev in beside:
        signal(barrier, land(cond, late), dev)
    for load in loads:
        load.start()
    count = number_of([land(cond, ~late) for cond, late, _ in beside])
    count = count + number_of([land(cond, ~above_late) for cond, _ in above_us]) + number_of([land(cond, ~below_late) for cond, _ in below_us])
    if far:
        signal(barrier, edge_u, by_way)
        count = count + pass_d.astype(jnp.int32)

    number = [0]

    def remote(src, dst, dev, arrival=None):
        i = number[0]
        number[0] += 1
        return pltpu.make_async_remote_copy(
            src_ref=src,
            dst_ref=dst,
            send_sem=send_sem.at[i],
            recv_sem=recv_sem.at[i if arrival is None else arrival],
            device_id=dev,
            device_id_type=MESH,
        )

    def all_of(*conds):
        return functools.reduce(land, conds)

    down, up = all_of(dyn, has_d), all_of(dyn, has_u)
    rest_down = rows_out.at[DIRECT:PLANES, rows - H :]
    rest_up = rows_out.at[DIRECT:PLANES, 0:H]
    down_sem = number[0]
    by_down = (land(down, ~edge_d) if far else down, up, remote(rest_down, rows_in.at[0, DIRECT:PLANES], {"gy": gy + 1}))
    to_below = [(down, up, remote(rows_out.at[0:DIRECT, rows - H :], rows_in.at[0, 0:DIRECT], {"gy": gy + 1})), by_down]
    to_above = [
        (up, down, remote(rows_out.at[0:DIRECT, 0:H], rows_in.at[1, 0:DIRECT], {"gy": gy - 1})),
        (up, down, remote(rest_up, rows_in.at[1, DIRECT:PLANES], {"gy": gy - 1})),
    ]
    passes, relays = [], []
    if far:
        passes = [(edge_d, pass_d, remote(rest_down, passing, by_way))]
        relays = [(pass_d, None, remote(passing, rows_in.at[0, DIRECT:PLANES], beyond, down_sem))]
    to_sides = [
        (all_of(dyn, has_r), all_of(dyn, has_l), remote(sides_out.at[0], sides_in.at[0], {"gx": gx + 1})),
        (all_of(dyn, has_l), all_of(dyn, has_r), remote(sides_out.at[1], sides_in.at[1], {"gx": gx - 1})),
    ]
    for side, (to, back, dx) in enumerate(((has_r, has_l, 1), (has_l, has_r, -1))):
        bottom = corners_out.at[side, :, rows - H :]
        top = corners_out.at[side, :, 0:H]
        to_below.append(
            (all_of(dyn, to, has_d), all_of(dyn, back, has_u), remote(bottom, corners_in.at[side, 0], {"gx": gx + dx, "gy": gy + 1}))
        )
        to_above.append(
            (all_of(dyn, to, has_u), all_of(dyn, back, has_d), remote(top, corners_in.at[side, 1], {"gx": gx + dx, "gy": gy - 1}))
        )
    halo = to_below + to_above + to_sides
    half = rows // 2
    mine = pl.multiple_of(half * core, half)
    other = pl.multiple_of(half * (1 - core), half)
    sibling = {"grp": me + 1 - 2 * core}
    to_sib = remote(block_sum.at[:, pl.ds(other, half)], sib, sibling)
    to_chips = [
        (chip + d < chips, chip - d >= 0, remote(chip_sum, lower.at[d - 1], {"grp": me + 2 * d})) for d in range(1, chips)
    ]
    to_rest = remote(part, rest, sibling)
    remap = [
        [
            (me > 0, me < n_grp - 1, remote(out.at[h, :, 0 : RIM * half], near.at[1, h], {"grp": me - 1})),
            (me < n_grp - 1, me > 0, remote(out.at[h, :, (levels - RIM) * half : levels * half], near.at[0, h], {"grp": me + 1})),
        ]
        for h in range(2)
    ]

    def start(item, when=None):
        @pl.when(item[0] if when is None else land(item[0], when))
        def _():
            item[2].start()

    def wait_recv(item):
        @pl.when(item[1])
        def _():
            item[2].wait_recv()

    def wait_send(item):
        @pl.when(item[0])
        def _():
            item[2].wait_send()

    @pl.when(count > 0)
    def _():
        pl.semaphore_wait(barrier, count)

    for cond, dev in above_us:
        signal(ready.at[0], land(cond, ~above_late), dev)
    for cond, dev in below_us:
        signal(ready.at[1], land(cond, ~below_late), dev)
    for cond, late, dev in aside:
        signal(ready.at[2], land(cond, ~late), dev)
    for cond, late, dev in same_tile:
        signal(ready.at[3], land(cond, ~late), dev)

    def await_ready(i, conds):
        n = number_of(conds)

        @pl.when(n > 0)
        def _():
            pl.semaphore_wait(ready.at[i], n)


    exps[...] = jnp.zeros(exps.shape, jnp.float32)
    for l in range(levels):
        for load in tiles[2 * l : 2 * l + 2]:
            load.wait()
        for c in range(5):
            cells = wide[c, tall_rows * l + H : tall_rows * l + H + rows, :]
            biggest = exponent(cells)
            exps[levels * c + l : levels * c + l + 1, :] = biggest
            rows_out[levels * c + l] = encode(cells, biggest)
    for i in range(2):
        held = exps[16 * i : 16 * i + 16, :]
        rows_out[20 + i] = jnp.concatenate([held, held], axis=0).astype(jnp.int32).astype(jnp.int16)

    for item in passes:
        start(item)
    for item in to_below[:2]:
        start(item, ~below_late)
    for item in to_above[:2]:
        start(item, ~above_late)

    lane = lane_ids(rows)
    for q in range(3):
        right = jnp.zeros((rows, 128), jnp.float32)
        left = jnp.zeros((rows, 128), jnp.float32)
        for c in (2 * q, 2 * q + 1):
            if c > 4:
                continue
            for l in range(levels):
                t = 2 * l + c % 2
                cells = wide[c, tall_rows * l + H : tall_rows * l + H + rows, :]
                here = lax.div(lane, 16) == t
                shift = (16 * t + 16) % 128
                right = jnp.where(here, pltpu.roll(cells, shift, 1) if shift else cells, right)
                shift = 16 * t
                left = jnp.where(here, pltpu.roll(cells, shift, 1) if shift else cells, left)
        for side, strip in enumerate((right, left)):
            biggest = exponent(strip)
            sides_out[side, q, 0:rows] = encode(strip, biggest)
            sides_out[side, q, rows : rows + 16] = jnp.broadcast_to(biggest, (16, 128)).astype(jnp.int32).astype(jnp.int16)
            corners_out[side, q] = strip.astype(jnp.bfloat16)

    for item in to_below[2:]:
        start(item, ~below_late)
    for item in to_above[2:]:
        start(item, ~above_late)
    for item, relay in zip(passes, relays):
        wait_recv(item)
        start(relay)
    await_ready(2, [land(cond, late) for cond, late, _ in aside])
    for item in to_sides:
        start(item)

    loads[0].wait()
    for f in range(gas.shape[0]):
        total = gas[f, 0].astype(jnp.float32)
        for l in range(1, levels):
            total = total + gas[f, l].astype(jnp.float32)
        block_sum[f] = total
    await_ready(3, [land(cond, late) for cond, late, _ in same_tile])
    to_sib.start()

    await_ready(0, [land(cond, below_late) for cond, _ in below_us])
    for item in to_below:
        start(item, below_late)

    def fill(cond, ref, *index, value=0):
        @pl.when(cond)
        def _():
            view = ref.at[index] if index else ref
            view[...] = jnp.full(view.shape, value, view.dtype)

    fill(~has_u, rows_in, 0)
    fill(~has_d, rows_in, 1)
    fill(~has_l, sides_in, 0)
    fill(~has_r, sides_in, 1)
    fill(~land(has_l, has_u), corners_in, 0, 0)
    fill(~land(has_l, has_d), corners_in, 0, 1)
    fill(~land(has_r, has_u), corners_in, 1, 0)
    fill(~land(has_r, has_d), corners_in, 1, 1)
    fill(me == 0, near, 0)
    fill(me == n_grp - 1, near, 1)
    for d in range(1, chips):
        fill(chip - d < 0, lower, d - 1, value=-4 * 8191)

    @pl.when(~dyn)
    def _():
        for c in range(3):
            for l in range(levels):
                for h in range(2):
                    at = tall_rows * l + H + half * h
                    out[h, c, half * l : half * l + half, :] = wide[c, at : at + half, :]

    for load in loads[1:]:
        load.wait()
    gases, gpoints = band.shape
    r0 = lax.broadcasted_iota(jnp.int32, (gpoints, gpoints), 0)
    r1 = lax.broadcasted_iota(jnp.int32, (gpoints, gpoints), 1)
    logs = jnp.log2(solar[...])
    high = logs.astype(jnp.bfloat16).astype(jnp.float32)
    middle = (logs - high).astype(jnp.bfloat16).astype(jnp.float32)
    low = logs - high - middle
    srcs = jnp.concatenate([band[...].astype(jnp.float32), high, middle, low], axis=0).astype(jnp.bfloat16)
    n_src = gases + 3
    l0 = lax.broadcasted_iota(jnp.int32, (rows, rows), 0)
    l1 = lax.broadcasted_iota(jnp.int32, (rows, rows), 1)
    lit_row = jnp.broadcast_to((route[...] < NDARK).astype(jnp.float32), (rows, rows))
    sunlit[...] = jnp.broadcast_to(jnp.sum(jnp.where(l0 == l1, lit_row, 0.0), axis=1, keepdims=True), (rows, 128))
    spread0 = lax.div(lax.broadcasted_iota(jnp.int32, (8 * gpoints, gpoints), 0), 8)
    spread1 = lax.broadcasted_iota(jnp.int32, (8 * gpoints, gpoints), 1)
    spread = (spread0 == spread1).astype(jnp.float32).astype(jnp.bfloat16)
    tall = lax.dot_general(spread, srcs, (((1,), (1,)), ((), ())), preferred_element_type=jnp.float32).astype(jnp.bfloat16)
    w0 = lax.broadcasted_iota(jnp.int32, (n_src, 128), 0)
    w1 = lax.broadcasted_iota(jnp.int32, (n_src, 128), 1)
    in_gas = w1 < 16 * gases
    owner = jnp.where(in_gas, lax.rem(lax.div(w1, 8), gases), w1 - 16 * gases + gases)
    widen = (w0 == owner).astype(jnp.float32).astype(jnp.bfloat16)
    spread_all = jnp.dot(tall, widen, preferred_element_type=jnp.float32)
    m0 = lax.broadcasted_iota(jnp.int32, (8 * gpoints, 128), 0)
    m1 = lax.broadcasted_iota(jnp.int32, (8 * gpoints, 128), 1)
    keep = (m1 >= 16 * gases) | (lax.rem(m0, 8) == lax.rem(m1, 8))
    lhs[...] = jnp.where(keep, spread_all, 0.0).astype(jnp.bfloat16)

    to_sib.wait_recv()
    both = block_sum[:, pl.ds(mine, half), :] + sib[...]
    chip_sum[...] = jnp.round((both - 4.0) * 8191.0).astype(jnp.int32).astype(jnp.int16)
    for item in to_chips:
        start(item)

    def radiate(start_row, ref):
        columns = []
        for g in range(half // 8):
            depth = ref[:, 8 * g : 8 * g + 8, :]
            for l in range(levels + 1):
                if l:
                    cells = gas[:, l - 1, pl.ds(start_row, half), :].astype(jnp.float32)
                    depth = depth + cells[:, 8 * g : 8 * g + 8, :]
                scaled = (depth * -LOG2E).reshape(8 * gases, 128)
                high = scaled.astype(jnp.bfloat16).astype(jnp.float32)
                stack = jnp.concatenate([high, scaled - high, jnp.ones((128 - 16 * gases, 128), jnp.float32)], axis=0)
                columns.append(stack.astype(jnp.bfloat16))
        cols = jnp.concatenate(columns, axis=1)
        expo = jnp.dot(lhs[...], cols, preferred_element_type=jnp.float32)
        flux = jnp.sum(jnp.exp2(expo).reshape(gpoints, 8, cols.shape[1]), axis=0)
        for l in range(levels):
            parts = []
            for g in range(half // 8):
                at = 128 * (g * (levels + 1) + l)
                parts.append(flux[:, at : at + 128] - flux[:, at + 128 : at + 256])
            diff = jnp.concatenate(parts, axis=0)
            lit = sunlit[pl.ds(start_row, half), :] > 0.5
            rate = diff / jnp.full((half, 128), mass[0, levels * me + l])
            heating[l, pl.ds(start_row, half), :] = jnp.where(lit, rate, 0.0)

    def shine():
        for item in to_chips:
            wait_recv(item)
        above = jnp.zeros(rest.shape, jnp.float32)
        for d in range(1, chips):
            above = above + (lower[d - 1].astype(jnp.int32).astype(jnp.float32) * (1.0 / 8191.0) + 4.0)
        even = (core == 0).astype(jnp.float32)
        part[...] = above + even * block_sum[:, pl.ds(mine, half), :]
        to_rest.start()
        prefix[...] = above + (1.0 - even) * sib[...]
        radiate(mine, prefix)
        to_rest.wait_recv()
        radiate(other, rest)

    waits = land(gy >= seam - 1, gy <= seam)

    @pl.when(waits)
    def _():
        shine()

    lane_h = lane_ids(rows + H)

    def decode_rows(i, at):
        exps[...] = jnp.concatenate([rows_in[i, 20], rows_in[i, 21]], axis=0).astype(jnp.int32).astype(jnp.float32)
        for c in range(5):
            for l in range(levels):
                k = levels * c + l
                wide[c, tall_rows * l + at : tall_rows * l + at + H, :] = decode(rows_in[i, k], exps[k : k + 1, :])

    def place_sides(q, strips, at):
        n = strips[0].shape[0]
        for c in (2 * q, 2 * q + 1):
            if c > 4:
                continue
            for l in range(levels):
                t = 2 * l + c % 2
                shift = (112 - 16 * t) % 128
                left = pltpu.roll(strips[0], shift, 1) if shift else strips[0]
                shift = (128 - 16 * t) % 128
                right = pltpu.roll(strips[1], shift, 1) if shift else strips[1]
                start_row = tall_rows * (levels + l) + at
                wide[c, start_row : start_row + n, :] = jnp.where(
                    lane_h[0:n] < 16, right, jnp.where(lane_h[0:n] >= 112, left, 0.0)
                )

    def send_levels(pair):
        start(pair[0], core == 0)
        start(pair[1])
        start(pair[0], core == 1)

    for item in to_above + to_sides:
        wait_recv(item)

    @pl.when(dyn)
    def _():
        decode_rows(1, H + rows)
        for q in range(3):
            strips = []
            for side in range(2):
                biggest = sides_in[side, q, rows : rows + 16].astype(jnp.int32).astype(jnp.float32)[0:1]
                middle = decode(sides_in[side, q, 0:rows], biggest)
                strips.append(jnp.concatenate([middle, corners_in[side, 1, q].astype(jnp.float32)], axis=0))
            place_sides(q, strips, H)
        prepare(wide, half, 0, half + 2 * H, p, fx, fy, bx, by, st)
        substeps(p, fx, fy, bx, by, st, out.at[1])

    send_levels(remap[1])
    await_ready(1, [land(cond, above_late) for cond, _ in above_us])
    for item in to_above:
        start(item, above_late)

    @pl.when(dyn)
    def _():
        prepare(wide, 0, H, half + 2 * H, p, fx, fy, bx, by, st)

    for item in to_below:
        wait_recv(item)

    @pl.when(dyn)
    def _():
        decode_rows(0, 0)
        for q in range(3):
            place_sides(q, [corners_in[side, 0, q].astype(jnp.float32) for side in range(2)], 0)
        prepare(wide, 0, 0, H, p, fx, fy, bx, by, st)
        substeps(p, fx, fy, bx, by, st, out.at[0])

    send_levels(remap[0])

    @pl.when(~waits)
    def _():
        shine()

    weights = []
    for kl in range(levels):
        k = levels * me + kl
        for o in range(-RIM, RIM + 1):
            w = jnp.float32(0)
            for j in range(ridx.shape[0]):
                w = w + jnp.where(ridx[j, k] == k + o, rweight[j, k], jnp.float32(0))
            weights.append(w)
    for h in (1, 0):
        for item in remap[h]:
            wait_recv(item)
        for kl in range(levels):
            for c in range(3):
                acc = jnp.zeros((half, 128), jnp.float32)
                for o in range(-RIM, RIM + 1):
                    m = kl + o
                    if m < 0:
                        cells = near[0, h, c, half * (m + RIM) : half * (m + RIM + 1), :]
                    elif m < levels:
                        cells = out[h, c, half * m : half * m + half, :]
                    else:
                        cells = near[1, h, c, half * (m - levels) : half * (m - levels + 1), :]
                    acc = acc + weights[(2 * RIM + 1) * kl + o + RIM] * cells
                new_state[c, kl, half * h : half * h + half, :] = acc

    for item in passes + relays + halo + to_chips + remap[0] + remap[1]:
        wait_send(item)
    to_sib.wait_send()
    to_rest.wait_send()


def shards(state, coefs, lagged_absorbers, sun_route, band_coef, solar, layer_mass, remap_index, remap_weight):
    sizes = tuple(lax.axis_size(a) for a in ("grp", "gx", "gy"))
    chips = sizes[0] // 2
    gases = lagged_absorbers.shape[0]
    levels, rows = state.shape[1:3]
    f32, bf16, i16 = jnp.float32, jnp.bfloat16, jnp.int16
    operands = (
        state, coefs, lagged_absorbers, sun_route.T, band_coef.T, solar.reshape(1, -1), layer_mass.reshape(1, -1),
        remap_index.T, remap_weight.T,
    )
    n_copies = 16 + 1 + (chips - 1) + 1 + 2
    return pl.pallas_call(
        functools.partial(kernel, sizes),
        out_shape=(jax.ShapeDtypeStruct(state.shape, f32), jax.ShapeDtypeStruct(state.shape[1:], f32)),
        in_specs=[pl.BlockSpec(memory_space=pltpu.HBM)] * len(operands),
        out_specs=(pl.BlockSpec(memory_space=pltpu.VMEM),) * 2,
        scratch_shapes=[
            pltpu.VMEM((1, rows), jnp.int32),
            pltpu.VMEM(band_coef.shape[::-1], bf16),
            pltpu.VMEM((1, solar.shape[0]), f32),
            pltpu.SMEM((1, layer_mass.shape[0]), f32),
            pltpu.SMEM(remap_index.shape[::-1], jnp.int32),
            pltpu.SMEM(remap_weight.shape[::-1], f32),
            pltpu.VMEM((5, 2 * levels * (rows + 2 * H), 128), f32),
            pltpu.VMEM(lagged_absorbers.shape, bf16),
            pltpu.VMEM((PLANES, rows, 128), i16),
            pltpu.VMEM((2, PLANES, H, 128), i16),
            pltpu.VMEM((2, 3, rows + 16, 128), i16),
            pltpu.VMEM((2, 3, rows + 16, 128), i16),
            pltpu.VMEM((2, 3, rows, 128), bf16),
            pltpu.VMEM((2, 2, 3, H, 128), bf16),
            pltpu.VMEM((32, 128), f32),
            pltpu.VMEM((2, 3, levels * rows, 128), f32),
            pltpu.VMEM((2, 2, 3, RIM * rows // 2, 128), f32),
            pltpu.VMEM((PLANES - DIRECT, H, 128), i16),
            *[pltpu.VMEM((rows // 2 + 2 * H, 2 * levels, 128), f32)] * 6,
            pltpu.VMEM((gases, rows, 128), f32),
            pltpu.VMEM((gases, rows // 2, 128), f32),
            pltpu.VMEM((gases, rows // 2, 128), i16),
            pltpu.VMEM((chips - 1, gases, rows // 2, 128), i16),
            pltpu.VMEM((gases, rows // 2, 128), f32),
            pltpu.VMEM((gases, rows // 2, 128), f32),
            pltpu.VMEM((gases, rows // 2, 128), f32),
            pltpu.VMEM((8 * band_coef.shape[0], 128), bf16),
            pltpu.VMEM((rows, 128), f32),
            pltpu.SemaphoreType.DMA((2, levels)),
            pltpu.SemaphoreType.DMA((7,)),
            pltpu.SemaphoreType.DMA((n_copies,)),
            pltpu.SemaphoreType.DMA((n_copies,)),
            pltpu.SemaphoreType.REGULAR((4,)),
        ],
        compiler_params=pltpu.CompilerParams(collective_id=0, has_side_effects=True, vmem_limit_bytes=40 * 2**20),
    )(
        *[pltpu.with_memory_space_constraint(a, pltpu.HBM) for a in operands]
    )


def solution(mesh):
    tiles = P(None, "grp", "gy", "gx")
    in_specs = (tiles, tiles, tiles, P("gy", "gx"), P(), P(), P(), P(), P())
    out_specs = (tiles, P("grp", "gy", "gx"))
    return jax.shard_map(shards, mesh=mesh, in_specs=in_specs, out_specs=out_specs, check_vma=False)
```
